512 devices in a mesh: row: 64 (over z_lo, y, x), col: 8 (over z_hi, core).
Axes of the slice: x: 4, y: 4, z: 16 (z_hi: 4, z_lo: 4; z = z_hi * 4 + z_lo), core: 2. Of those that a mesh axis runs over, the one named last changes fastest.
Arguments:
- left: bfloat16 [128, 1024, 1024], P(None, 'row', 'col'), may hold values from -6 to 6
- right: bfloat16 [128, 1024, 1024], P(None, 'row', 'col'), may hold values from -6 to 6
- gate_out: bfloat16 [128, 1024, 1024], P(None, 'row', 'col'), may hold values from 0.019897461 to 1
- out_grad: bfloat16 [128, 1024, 1024], P(None, 'row', 'col'), may hold values from -6 to 6
- norm_gain: float32 [128], replicated, may hold values from 0.1 to 1.9
- out_weight: bfloat16 [128, 128], replicated, may hold values from -0.5 to 0.5
- token_mask: int32 [1024], replicated, may hold values 0 or 1
Outputs:
- left_grad: bfloat16 [128, 1024, 1024], P(None, 'row', 'col')
- right_grad: bfloat16 [128, 1024, 1024], P(None, 'row', 'col')
The draws below stay inside these ranges and needn't reach their ends.
Inputs may be any that keep to these rules, and one draw needn't show every extreme that they name: `token_mask`: 1 marks a real token, 0 a padding token.
All inputs are finite; a program needn't handle non-finite values.
Results may differ from the reference program's by a relative error of at most 0.0058.
Values may be sent and summed in bfloat16 or wider, within the bound.
No kernel may reach another device: no remote copies, remote signals or barrier semaphores. Data moves between devices by JAX's collectives and lax.ppermute only.
A program may use at most 64 MiB of HBM per device.

```python
import jax
import jax.numpy as jnp
from jax import lax

C_PAIR = 128
HIDDEN_SIZE = 128
TOKENS = 1024


def touch_ends(values, stream_key, least, largest):
    index_at = [jax.random.randint(jax.random.fold_in(stream_key, axis), (), 0, length) for axis, length in enumerate(values.shape)]
    main_axis = values.shape.index(max(values.shape))
    neighbour = index_at[:main_axis] + [(index_at[main_axis] + 1) % values.shape[main_axis]] + index_at[main_axis + 1:]
    return values.at[tuple(index_at)].set(least).at[tuple(neighbour)].set(largest)


def steps_of(key, dims, pieces, low, largest):
    def one(axis_at, blocks):
        draws = jax.random.uniform(jax.random.fold_in(jax.random.fold_in(key, 6), axis_at), (blocks,), jnp.float32, low / len(pieces), largest / len(pieces))
        return jnp.repeat(jnp.exp(draws), dims[axis_at] // blocks).reshape((-1,) + (1,) * (len(dims) - axis_at - 1))

    factor_of = one(*pieces[0])
    for cut in pieces[1:]:
        factor_of = factor_of * one(*cut)
    return factor_of


def gaussian(key, extent, spread, bound, cuts=(), kind=jnp.bfloat16):
    drawn = spread * jax.random.normal(key, extent, jnp.float32)
    if cuts:
        drawn = drawn * steps_of(key, extent, cuts, -0.22, 0.18)
    return jnp.clip(drawn, -bound, bound).astype(kind)


def setup_inputs(seed: int = 0) -> dict:
    streams_of = jax.random.split(jax.random.key(seed), 8)
    return {
        "left": gaussian(streams_of[0], (HIDDEN_SIZE, TOKENS, TOKENS), 1.0, 6.0, ((1, 64), (2, 8))),
        "right": gaussian(streams_of[1], (HIDDEN_SIZE, TOKENS, TOKENS), 1.0, 6.0, ((1, 64), (2, 8))),
        "gate_out": jnp.clip(0.019897461 + 0.98010254 * jax.random.uniform(streams_of[2], (C_PAIR, TOKENS, TOKENS), jnp.float32) ** steps_of(streams_of[2], (C_PAIR, TOKENS, TOKENS), ((1, 64), (2, 8)), -0.2, 0.2), 0.019897461, 1.0).astype(jnp.bfloat16),
        "out_grad": gaussian(streams_of[3], (C_PAIR, TOKENS, TOKENS), 1.0, 6.0, ((1, 64), (2, 8))),
        "norm_gain": jnp.clip(1.0 + 0.18 * jax.random.normal(streams_of[4], (HIDDEN_SIZE,), jnp.float32), 0.1, 1.9),
        "out_weight": gaussian(streams_of[5], (HIDDEN_SIZE, C_PAIR), HIDDEN_SIZE ** -0.5, 0.5),
        "token_mask": touch_ends((jax.random.randint(streams_of[6], (TOKENS,), 0, 8) < 7).astype(jnp.int32), jax.random.fold_in(streams_of[6], 1), 0, 1),
    }


norm_eps = 1e-05

def one_product(pair_args):
    left_one, right_one = pair_args
    return jnp.dot(left_one.astype(jnp.float32), right_one.astype(jnp.float32).T, precision=lax.Precision.HIGHEST).astype(jnp.bfloat16)

def one_left_grad(pair_args):
    grad_one, right_one = pair_args
    return jnp.dot(grad_one.astype(jnp.float32), right_one.astype(jnp.float32), precision=lax.Precision.HIGHEST).astype(jnp.bfloat16)

def one_right_grad(pair_args):
    grad_one, left_one = pair_args
    return jnp.dot(grad_one.astype(jnp.float32).T, left_one.astype(jnp.float32), precision=lax.Precision.HIGHEST).astype(jnp.bfloat16)

def reference(left, right, gate_out, out_grad, norm_gain, out_weight, token_mask):
    mask_float = token_mask.astype(jnp.float32)
    pair_mask = (mask_float[:, None] * mask_float[None, :]).astype(jnp.bfloat16)[None]
    left_masked = left * pair_mask
    right_masked = right * pair_mask
    product = lax.map(one_product, (left_masked, right_masked))
    floats = product.astype(jnp.float32)
    center = floats - lax.optimization_barrier(jnp.mean(floats, axis=0, keepdims=True))
    inv_std = lax.rsqrt(lax.optimization_barrier(jnp.mean(center * center, axis=0, keepdims=True)) + norm_eps)
    normed = center * inv_std
    gated_grad = (gate_out.astype(jnp.float32) * out_grad.astype(jnp.float32)).astype(jnp.bfloat16)
    linear = jnp.dot(out_weight, gated_grad.reshape(C_PAIR, -1), preferred_element_type=jnp.float32)
    linear = linear.reshape(HIDDEN_SIZE, TOKENS, TOKENS)
    scaled = norm_gain[:, None, None] * linear
    prod_grad = inv_std * (scaled - lax.optimization_barrier(jnp.mean(scaled, axis=0, keepdims=True)) - normed * lax.optimization_barrier(jnp.mean(scaled * normed, axis=0, keepdims=True)))
    prod_grad = prod_grad.astype(jnp.bfloat16)
    left_grad = lax.map(one_left_grad, (prod_grad, right_masked)) * pair_mask
    right_grad = lax.map(one_right_grad, (prod_grad, left_masked)) * pair_mask
    return (left_grad, right_grad)
```

```python
import functools

import jax
import jax.numpy as jnp
from jax import lax
from jax.experimental import pallas as pl
from jax.experimental.pallas import tpu as pltpu
from jax.sharding import Mesh, PartitionSpec as P

norm_eps = 1e-05

AXES = ("zl", "y", "xh", "xl", "zh", "c")
SIZES = (4, 4, 2, 2, 4, 2)
ROW = ("zl", "y", "xh", "xl")
COL = ("zh", "c")
OWNERS = ("zl", "y", "xh", "zh")
BF16 = jnp.bfloat16
F32 = jnp.float32
VMEM_LIMIT = 32 * 1024 * 1024


def gather_left(both_ref):
    return jnp.concatenate(
        [both_ref[:, z, 0:16, :].reshape(512, 128) for z in range(4)], axis=1
    )


def fill_right(x_lo, both_ref, other_ref, right):
    for z in range(4):
        cols = slice(z * 128, (z + 1) * 128)
        mine = both_ref[:, z, 16:32, :].reshape(4, 2, 4, 16, 128)
        other = other_ref[:, z, :, :].reshape(4, 2, 4, 16, 128)
        for yh in range(2):
            right[yh, :, :, x_lo, :, cols] = mine[:, yh]
            right[yh, :, :, 1 - x_lo, :, cols] = other[:, yh]


def product_kernel(place_ref, both_ref, other_ref, keep_ref, send_ref, right):
    x_lo, core = place_ref[0], place_ref[1]
    fill_right(x_lo, both_ref, other_ref, right)
    left = gather_left(both_ref)
    for out_ref, which in ((keep_ref, core), (send_ref, 1 - core)):
        part = lax.dot_general(
            left,
            right[which].reshape(512, 512),
            (((1,), (1,)), ((), ())),
            preferred_element_type=F32,
        )
        for z in range(4):
            out_ref[:, z, :, :] = (
                part[:, z * 128 : (z + 1) * 128].reshape(32, 16, 128).astype(out_ref.dtype)
            )


def grads_kernel(
    place_ref, both_ref, other_ref, grad_ref, grad_other_ref, left_ref, keep_ref, send_ref, right, grad, parts
):
    x_lo, core = place_ref[0], place_ref[1]
    fill_right(x_lo, both_ref, other_ref, right)
    left = gather_left(both_ref)
    for z in range(4):
        cols = slice(z * 128, (z + 1) * 128)
        grad[core, :, :, cols] = grad_ref[:, z, :, :]
        grad[1 - core, :, :, cols] = grad_other_ref[:, z, :, :]
    total = jnp.zeros((512, 512), F32)
    for which in range(2):
        block = grad[which].reshape(512, 512)
        total += jnp.dot(block, right[which].reshape(512, 512), preferred_element_type=F32)
        part = lax.dot_general(
            block, left, (((0,), (0,)), ((), ())), preferred_element_type=F32
        ).reshape(4, 4, 2, 16, 512)
        for half in range(2):
            parts[half, :, which] = part[:, :, half]
    for z in range(4):
        cols = slice(z * 128, (z + 1) * 128)
        left_ref[:, z, :, :] = total[:, cols].reshape(32, 16, 128).astype(BF16)
        keep_ref[:, z, :, :] = parts[x_lo, :, :, :, :, cols].reshape(32, 16, 128)
        send_ref[:, z, :, :] = parts[1 - x_lo, :, :, :, :, cols].reshape(32, 16, 128).astype(BF16)


def norm_kernel(product_ref, scaled_ref, grad_ref):
    count = product_ref.shape[0]

    def load(c):
        return product_ref[c].astype(F32)

    zeros = jnp.zeros(product_ref.shape[1:], F32)

    def sums(c, carry):
        return carry[0] + load(c), carry[1] + scaled_ref[c]

    total, scaled_total = lax.fori_loop(0, count, sums, (zeros, zeros), unroll=8)
    mean = total * (1.0 / count)
    scaled_mean = scaled_total * (1.0 / count)

    def squares(c, carry):
        center = load(c) - mean
        return carry[0] + center * center, carry[1] + scaled_ref[c] * center

    square, cross = lax.fori_loop(0, count, squares, (zeros, zeros), unroll=8)
    inv_std = lax.rsqrt(square * (1.0 / count) + norm_eps)
    slope = inv_std * inv_std * cross * (1.0 / count)

    def write(c, carry):
        center = load(c) - mean
        grad_ref[c] = (inv_std * (scaled_ref[c] - scaled_mean - center * slope)).astype(BF16)
        return carry

    lax.fori_loop(0, count, write, 0, unroll=8)


def vmem():
    return pl.BlockSpec(memory_space=pltpu.VMEM)


def smem():
    return pl.BlockSpec(memory_space=pltpu.SMEM)


def blocks(dtype):
    return jax.ShapeDtypeStruct((32, 4, 16, 128), dtype)


def call(kernel, outs, operands, scratch, flops, scalars=1):
    moved = sum(o.size * o.dtype.itemsize for o in (*operands, *outs))
    return pl.pallas_call(
        kernel,
        out_shape=outs,
        in_specs=[smem()] * scalars + [vmem()] * (len(operands) - scalars),
        out_specs=[vmem()] * len(outs),
        scratch_shapes=scratch,
        compiler_params=pltpu.CompilerParams(vmem_limit_bytes=VMEM_LIMIT),
        cost_estimate=pl.CostEstimate(flops=flops, bytes_accessed=moved, transcendentals=0),
    )(*operands)


def swap(x, axis):
    return lax.ppermute(x, axis, [(0, 1), (1, 0)])


def to_owners(x):
    return lax.all_to_all(x, OWNERS, split_axis=0, concat_axis=0, tiled=True)


def on_device(left, right, gate_out, out_grad, norm_gain, out_weight, token_mask):
    row_count, col_count = left.shape[1:]
    row_start = lax.axis_index(ROW) * row_count
    col_start = lax.axis_index(COL) * col_count
    mask_float = token_mask.astype(F32)
    row_mask = lax.dynamic_slice_in_dim(mask_float, row_start, row_count)
    col_mask = lax.dynamic_slice_in_dim(mask_float, col_start, col_count)
    tile_mask = (row_mask[:, None] * col_mask[None, :]).astype(BF16)[None]
    place = jnp.stack([lax.axis_index("xl"), lax.axis_index("c")]).astype(jnp.int32)

    both = to_owners(jnp.concatenate([left * tile_mask, right * tile_mask], axis=1))

    gated_grad = (gate_out.astype(F32) * out_grad.astype(F32)).astype(BF16)
    linear = jnp.dot(
        out_weight, gated_grad.reshape(gated_grad.shape[0], -1), preferred_element_type=F32
    )
    scaled = norm_gain[:, None, None] * linear.reshape(left.shape)

    both = both.reshape(32, 4, 32, 128)
    other = swap(both[:, :, 16:, :], "xl")
    flops = 2 * 512 * 512 * 1024
    right_scratch = pltpu.VMEM((2, 4, 4, 2, 16, 512), BF16)
    keep, send = call(
        product_kernel, [blocks(F32), blocks(BF16)], [place, both, other], [right_scratch], flops
    )
    product = (keep + swap(send, "c").astype(F32)).astype(BF16)
    product = to_owners(product.reshape(128, 16, 128))

    (grad,) = call(
        norm_kernel,
        [jax.ShapeDtypeStruct(product.shape, BF16)],
        [product, scaled],
        [],
        20 * product.size,
        scalars=0,
    )
    grad = to_owners(grad).reshape(32, 4, 16, 128)
    left_sum, keep, send = call(
        grads_kernel,
        [blocks(BF16), blocks(F32), blocks(BF16)],
        [place, both, other, grad, swap(grad, "c")],
        [
            right_scratch,
            pltpu.VMEM((2, 32, 16, 512), BF16),
            pltpu.VMEM((2, 4, 2, 4, 16, 512), F32),
        ],
        2 * flops,
    )
    right_sum = (keep + swap(send, "xl").astype(F32)).astype(BF16)
    sums = jnp.concatenate([left_sum, right_sum], axis=2).reshape(128, 32, 128)
    home = to_owners(sums)
    return (home[:, :16] * tile_mask, home[:, 16:] * tile_mask)


def solution(mesh):
    fine = Mesh(mesh.devices.reshape(SIZES), AXES)
    tile = P(None, ROW, COL)
    return jax.shard_map(
        on_device,
        mesh=fine,
        in_specs=(tile, tile, tile, tile, P(), P(), P()),
        out_specs=(tile, tile),
        check_vma=False,
    )
```

```python
import jax
import jax.numpy as jnp
from jax import lax
from jax.experimental import pallas as pl
from jax.experimental.pallas import tpu as pltpu
from jax.sharding import Mesh, PartitionSpec as P

norm_eps = 1e-05

AXES = ("zl", "y", "xh", "xl", "zh", "c")
SIZES = (4, 4, 2, 2, 4, 2)
ROW = ("zl", "y", "xh", "xl")
COL = ("zh", "c")
PAIR = "xh"
OWNERS = ("zl", "y", "xl", "zh")
BF16 = jnp.bfloat16
F32 = jnp.float32
VMEM_LIMIT = 32 * 1024 * 1024


def lanes(z, half=0):
    return slice(512 * half + 128 * z, 512 * half + 128 * (z + 1))


def whole_left(both_ref, left_other_ref):
    parts = [both_ref[:, z, 0:16, :].reshape(512, 128) for z in range(4)]
    parts += [left_other_ref[:, z, :, :].reshape(512, 128) for z in range(4)]
    return jnp.concatenate(parts, axis=1)


def whole_grad(grad_ref):
    return jnp.concatenate([grad_ref[:, z, :, :].reshape(512, 128) for z in range(4)], axis=1)


def product_kernel(
    place_ref, both_ref, left_other_ref, mine_ref, other_ref, far_mine_ref, far_other_ref, out_ref, right_ref
):
    pair = place_ref[0]
    for z in range(4):
        for half, (near, far) in enumerate(((mine_ref, far_mine_ref), (other_ref, far_other_ref))):
            cols = lanes(z, half)
            right_ref[:, :, pair, :, :, cols] = near[:, z, :, :].reshape(4, 2, 2, 16, 128)
            right_ref[:, :, 1 - pair, :, :, cols] = far[:, z, :, :].reshape(4, 2, 2, 16, 128)
    product = lax.dot_general(
        whole_left(both_ref, left_other_ref),
        right_ref[...].reshape(512, 1024),
        (((1,), (1,)), ((), ())),
        preferred_element_type=F32,
    )
    for z in range(4):
        out_ref[:, z, :, :] = product[:, lanes(z)].reshape(32, 16, 128).astype(BF16)


def right_grad_kernel(place_ref, both_ref, left_other_ref, grad_ref, send_other_ref, send_mine_ref, keep_ref, parts):
    pair = place_ref[0]
    part = lax.dot_general(
        whole_grad(grad_ref),
        whole_left(both_ref, left_other_ref),
        (((0,), (0,)), ((), ())),
        preferred_element_type=F32,
    ).reshape(8, 2, 2, 16, 1024)
    for bit in range(2):
        parts[bit] = part[:, bit]
    for z in range(4):
        for half, send_ref in enumerate((send_mine_ref, send_other_ref)):
            cols = lanes(z, half)
            send_ref[:, z, :, :] = parts[1 - pair, :, :, :, cols].reshape(16, 16, 128).astype(BF16)
            keep_ref[half, :, z, :, :] = parts[pair, :, :, :, cols].reshape(16, 16, 128)


def left_grad_kernel(grad_ref, right_ref, send_ref, keep_ref):
    part = jnp.dot(
        whole_grad(grad_ref), right_ref[...].reshape(512, 1024), preferred_element_type=F32
    )
    for z in range(4):
        keep_ref[:, z, :, :] = part[:, lanes(z)].reshape(32, 16, 128)
        send_ref[:, z, :, :] = part[:, lanes(z, 1)].reshape(32, 16, 128).astype(BF16)


def gather_kernel(place_ref, left_keep_ref, left_got_ref, right_keep_ref, right_got_ref, right_other_ref, out_ref):
    core = place_ref[1]
    out_ref[:, :, :, :, 0:16, :] = (
        (left_keep_ref[...] + left_got_ref[...].astype(F32)).astype(BF16).reshape(4, 2, 4, 4, 16, 128)
    )
    out_ref[:, core, :, :, 16:32, :] = (
        (right_keep_ref[...] + right_got_ref[...].astype(F32)).astype(BF16).reshape(4, 4, 4, 16, 128)
    )
    out_ref[:, 1 - core, :, :, 16:32, :] = right_other_ref[...].reshape(4, 4, 4, 16, 128)


def norm_kernel(product_ref, scaled_ref, grad_ref):
    count = product_ref.shape[0]

    def load(c):
        return product_ref[c].astype(F32)

    zeros = jnp.zeros(product_ref.shape[1:], F32)

    def sums(c, carry):
        return carry[0] + load(c), carry[1] + scaled_ref[c]

    total, scaled_total = lax.fori_loop(0, count, sums, (zeros, zeros), unroll=8)
    mean = total * (1.0 / count)
    scaled_mean = scaled_total * (1.0 / count)

    def squares(c, carry):
        center = load(c) - mean
        return carry[0] + center * center, carry[1] + scaled_ref[c] * center

    square, cross = lax.fori_loop(0, count, squares, (zeros, zeros), unroll=8)
    inv_std = lax.rsqrt(square * (1.0 / count) + norm_eps)
    slope = inv_std * inv_std * cross * (1.0 / count)

    def write(c, carry):
        center = load(c) - mean
        grad_ref[c] = (inv_std * (scaled_ref[c] - scaled_mean - center * slope)).astype(BF16)
        return carry

    lax.fori_loop(0, count, write, 0, unroll=8)


def vmem():
    return pl.BlockSpec(memory_space=pltpu.VMEM)


def smem():
    return pl.BlockSpec(memory_space=pltpu.SMEM)


def shape(dims, dtype):
    return jax.ShapeDtypeStruct(dims, dtype)


def call(kernel, outs, operands, scratch=(), flops=0, scalars=1):
    moved = sum(o.size * o.dtype.itemsize for o in (*operands, *outs))
    return pl.pallas_call(
        kernel,
        out_shape=outs,
        in_specs=[smem()] * scalars + [vmem()] * (len(operands) - scalars),
        out_specs=[vmem()] * len(outs),
        scratch_shapes=scratch,
        compiler_params=pltpu.CompilerParams(vmem_limit_bytes=VMEM_LIMIT),
        cost_estimate=pl.CostEstimate(flops=flops, bytes_accessed=moved, transcendentals=0),
    )(*operands)


def swap(x, axis):
    return lax.ppermute(x, axis, [(0, 1), (1, 0)])


def to_owners(x):
    return lax.all_to_all(x, OWNERS, split_axis=0, concat_axis=0, tiled=True)


def on_device(left, right, gate_out, out_grad, norm_gain, out_weight, token_mask):
    row_count, col_count = left.shape[1:]
    row_start = lax.axis_index(ROW) * row_count
    col_start = lax.axis_index(COL) * col_count
    row_mask = lax.dynamic_slice_in_dim(token_mask, row_start, row_count)
    col_mask = lax.dynamic_slice_in_dim(token_mask, col_start, col_count)
    tile_mask = (row_mask[:, None] * col_mask[None, :]).astype(BF16)[None]
    core = lax.axis_index("c")
    place = jnp.stack([lax.axis_index(PAIR), core]).astype(jnp.int32)

    both = to_owners(jnp.concatenate([left * tile_mask, right * tile_mask], axis=1))
    both, gate_out, out_grad = lax.optimization_barrier((both, gate_out, out_grad))

    rows = both.reshape(4, 2, 4, 4, 32, 128)[:, :, :, :, 16:, :]
    mine = lax.dynamic_index_in_dim(rows, core, 1, keepdims=False).reshape(16, 4, 16, 128)
    far_mine = swap(mine, PAIR)
    other = swap(lax.dynamic_index_in_dim(rows, 1 - core, 1, keepdims=False).reshape(16, 4, 16, 128), "c")
    far_other = swap(other, PAIR)
    both = both.reshape(32, 4, 32, 128)
    left_other = swap(both[:, :, :16, :], "c")

    gated_grad = (gate_out.astype(F32) * out_grad.astype(F32)).astype(BF16)
    linear = jnp.dot(
        out_weight, gated_grad.reshape(gated_grad.shape[0], -1), preferred_element_type=F32
    )
    scaled = norm_gain[:, None, None] * linear.reshape(left.shape)
    far_other, scaled = lax.optimization_barrier((far_other, scaled))

    flops = 2 * 512 * 512 * 1024
    blocks = (32, 4, 16, 128)
    product, right_whole = call(
        product_kernel,
        [shape(blocks, BF16), shape((4, 2, 2, 2, 16, 1024), BF16)],
        [place, both, left_other, mine, other, far_mine, far_other],
        flops=flops,
    )
    product = to_owners(product.reshape(left.shape))
    (grad,) = call(
        norm_kernel,
        [shape(left.shape, BF16)],
        [product, scaled],
        flops=20 * product.size,
        scalars=0,
    )
    grad = to_owners(grad).reshape(blocks)

    half = (16, 4, 16, 128)
    send_other, send_mine, keep = call(
        right_grad_kernel,
        [shape(half, BF16), shape(half, BF16), shape((2, *half), F32)],
        [place, both, left_other, grad],
        [pltpu.VMEM((2, 8, 2, 16, 1024), F32)],
        flops=flops,
    )
    right_other = (keep[1] + swap(send_other, PAIR).astype(F32)).astype(BF16)
    right_got = swap(send_mine, PAIR)
    left_send, left_keep = call(
        left_grad_kernel, [shape(blocks, BF16), shape(blocks, F32)], [grad, right_whole], flops=flops, scalars=0
    )
    (sums,) = call(
        gather_kernel,
        [shape((4, 2, 4, 4, 32, 128), BF16)],
        [place, left_keep, swap(left_send, "c"), keep[0], right_got, swap(right_other, "c")],
    )
    home = to_owners(sums.reshape(128, 32, 128))
    return (home[:, :16] * tile_mask, home[:, 16:] * tile_mask)


def solution(mesh):
    fine = Mesh(mesh.devices.reshape(SIZES), AXES)
    tile = P(None, ROW, COL)
    return jax.shard_map(
        on_device,
        mesh=fine,
        in_specs=(tile, tile, tile, tile, P(), P(), P()),
        out_specs=(tile, tile),
        check_vma=False,
    )
```

```python
import jax
import jax.numpy as jnp
from jax import lax
from jax.experimental import pallas as pl
from jax.experimental.pallas import tpu as pltpu
from jax.sharding import Mesh, PartitionSpec as P

norm_eps = 1e-05

AXES = ("zl", "y", "xh", "xl", "zh", "c")
SIZES = (4, 4, 2, 2, 4, 2)
ROW = ("zl", "y", "xh", "xl")
COL = ("zh", "c")
PAIR = "xh"
OWNERS = ("zl", "y", "xl", "zh")
BF16 = jnp.bfloat16
F32 = jnp.float32
VMEM_LIMIT = 32 * 1024 * 1024


def lanes(z, half=0):
    return slice(512 * half + 128 * z, 512 * half + 128 * (z + 1))


def whole_left(both_ref, left_other_ref):
    parts = [both_ref[:, z, 0:16, :].reshape(512, 128) for z in range(4)]
    parts += [left_other_ref[:, z, :, :].reshape(512, 128) for z in range(4)]
    return jnp.concatenate(parts, axis=1)


def whole_grad(grad_ref):
    return jnp.concatenate([grad_ref[:, z, :, :].reshape(512, 128) for z in range(4)], axis=1)


def product_kernel(
    place_ref, both_ref, left_other_ref, near_ref, far_0_ref, far_1_ref, out_ref, right_ref
):
    pair, core = place_ref[0], place_ref[1]

    def place(near, source):
        for z in range(4):
            for half in range(2):
                rows = source[half, :, z, :, :].reshape(4, 2, 2, 16, 128)
                right_ref[:, :, near, :, :, lanes(z, half)] = rows

    place(pair, near_ref)

    @pl.when(core == 0)
    def _():
        place(1 - pair, far_0_ref)

    @pl.when(core == 1)
    def _():
        place(1 - pair, far_1_ref)

    product = lax.dot_general(
        whole_left(both_ref, left_other_ref),
        right_ref[...].reshape(512, 1024),
        (((1,), (1,)), ((), ())),
        preferred_element_type=F32,
    )
    for z in range(4):
        out_ref[:, z, :, :] = product[:, lanes(z)].reshape(32, 16, 128).astype(BF16)


def grads_kernel(
    place_ref, both_ref, left_other_ref, grad_ref, right_ref,
    send_other_ref, send_mine_ref, keep_ref, left_send_ref, left_keep_ref, parts,
):
    pair = place_ref[0]
    grad = whole_grad(grad_ref)
    part = lax.dot_general(
        grad,
        whole_left(both_ref, left_other_ref),
        (((0,), (0,)), ((), ())),
        preferred_element_type=F32,
    ).reshape(8, 2, 2, 16, 1024)
    for bit in range(2):
        parts[bit] = part[:, bit]
    for z in range(4):
        for half, send_ref in enumerate((send_mine_ref, send_other_ref)):
            cols = lanes(z, half)
            send_ref[:, z, :, :] = parts[1 - pair, :, :, :, cols].reshape(16, 16, 128).astype(BF16)
            keep_ref[half, :, z, :, :] = parts[pair, :, :, :, cols].reshape(16, 16, 128)
    part = jnp.dot(grad, right_ref[...].reshape(512, 1024), preferred_element_type=F32)
    for z in range(4):
        left_keep_ref[:, z, :, :] = part[:, lanes(z)].reshape(32, 16, 128)
        left_send_ref[:, z, :, :] = part[:, lanes(z, 1)].reshape(32, 16, 128).astype(BF16)


def gather_kernel(place_ref, left_keep_ref, left_got_ref, right_keep_ref, right_got_ref, right_other_ref, out_ref):
    core = place_ref[1]
    out_ref[:, :, :, :, 0:16, :] = (
        (left_keep_ref[...] + left_got_ref[...].astype(F32)).astype(BF16).reshape(4, 2, 4, 4, 16, 128)
    )
    out_ref[:, core, :, :, 16:32, :] = (
        (right_keep_ref[...] + right_got_ref[...].astype(F32)).astype(BF16).reshape(4, 4, 4, 16, 128)
    )
    out_ref[:, 1 - core, :, :, 16:32, :] = right_other_ref[...].reshape(4, 4, 4, 16, 128)


def norm_kernel(product_ref, scaled_ref, grad_ref):
    count = product_ref.shape[0]

    def load(c):
        return product_ref[c].astype(F32)

    zeros = jnp.zeros(product_ref.shape[1:], F32)

    def sums(c, carry):
        return carry[0] + load(c), carry[1] + scaled_ref[c]

    total, scaled_total = lax.fori_loop(0, count, sums, (zeros, zeros), unroll=8)
    mean = total * (1.0 / count)
    scaled_mean = scaled_total * (1.0 / count)

    def squares(c, carry):
        center = load(c) - mean
        return carry[0] + center * center, carry[1] + scaled_ref[c] * center

    square, cross = lax.fori_loop(0, count, squares, (zeros, zeros), unroll=8)
    inv_std = lax.rsqrt(square * (1.0 / count) + norm_eps)
    slope = inv_std * inv_std * cross * (1.0 / count)

    def write(c, carry):
        center = load(c) - mean
        grad_ref[c] = (inv_std * (scaled_ref[c] - scaled_mean - center * slope)).astype(BF16)
        return carry

    lax.fori_loop(0, count, write, 0, unroll=8)


def vmem():
    return pl.BlockSpec(memory_space=pltpu.VMEM)


def smem():
    return pl.BlockSpec(memory_space=pltpu.SMEM)


def shape(dims, dtype):
    return jax.ShapeDtypeStruct(dims, dtype)


def call(kernel, outs, operands, scratch=(), flops=0, scalars=1):
    moved = sum(o.size * o.dtype.itemsize for o in (*operands, *outs))
    return pl.pallas_call(
        kernel,
        out_shape=outs,
        in_specs=[smem()] * scalars + [vmem()] * (len(operands) - scalars),
        out_specs=[vmem()] * len(outs),
        scratch_shapes=scratch,
        compiler_params=pltpu.CompilerParams(vmem_limit_bytes=VMEM_LIMIT),
        cost_estimate=pl.CostEstimate(flops=flops, bytes_accessed=moved, transcendentals=0),
    )(*operands)


def swap(x, axis):
    return lax.ppermute(x, axis, [(0, 1), (1, 0)])


def swap_pair(x, core):
    at = [2 * bit + core for bit in range(2)]
    return lax.ppermute(x, (PAIR, "c"), [(at[0], at[1]), (at[1], at[0])])


def to_owners(x):
    return lax.all_to_all(x, OWNERS, split_axis=0, concat_axis=0, tiled=True)


def on_device(left, right, gate_out, out_grad, norm_gain, out_weight, token_mask):
    core = lax.axis_index("c")
    place = jnp.stack([lax.axis_index(PAIR), core]).astype(jnp.int32)
    row_count, col_count = left.shape[1:]
    mask_float = token_mask.astype(F32)
    row_mask = lax.dynamic_slice_in_dim(mask_float, lax.axis_index(ROW) * row_count, row_count)
    col_mask = lax.dynamic_slice_in_dim(mask_float, lax.axis_index(COL) * col_count, col_count)
    tile_mask = (row_mask[:, None] * col_mask[None, :]).astype(BF16)[None]

    both = to_owners(jnp.concatenate([left * tile_mask, right * tile_mask], axis=1))

    rows = both.reshape(4, 2, 4, 4, 32, 128)[:, :, :, :, 16:, :]
    half = (16, 4, 16, 128)
    mine = lax.dynamic_index_in_dim(rows, core, 1, keepdims=False).reshape(half)
    other = swap(lax.dynamic_index_in_dim(rows, 1 - core, 1, keepdims=False).reshape(half), "c")
    near = jnp.stack([mine, other])
    both = both.reshape(32, 4, 32, 128)
    left_mine, near, gate_out, out_grad = lax.optimization_barrier((both[:, :, :16, :], near, gate_out, out_grad))
    far_1 = swap_pair(near, 1)
    left_other = swap(left_mine, "c")

    gated_grad = (gate_out.astype(F32) * out_grad.astype(F32)).astype(BF16)
    linear = jnp.dot(
        out_weight, gated_grad.reshape(gated_grad.shape[0], -1), preferred_element_type=F32
    )
    scaled = norm_gain[:, None, None] * linear.reshape(left.shape)
    near_0, far_1, left_other, scaled = lax.optimization_barrier((near, far_1, left_other, scaled))
    far_0 = swap_pair(near_0, 0)

    flops = 2 * 512 * 512 * 1024
    blocks = (32, 4, 16, 128)
    product, right_whole = call(
        product_kernel,
        [shape(blocks, BF16), shape((4, 2, 2, 2, 16, 1024), BF16)],
        [place, both, left_other, near, far_0, far_1],
        flops=flops,
    )
    product = to_owners(product.reshape(left.shape))
    (grad,) = call(
        norm_kernel,
        [shape(left.shape, BF16)],
        [product, scaled],
        flops=20 * product.size,
        scalars=0,
    )
    grad = to_owners(grad).reshape(blocks)

    half = (16, 4, 16, 128)
    send_other, send_mine, keep, left_send, left_keep = call(
        grads_kernel,
        [shape(half, BF16), shape(half, BF16), shape((2, *half), F32), shape(blocks, BF16), shape(blocks, F32)],
        [place, both, left_other, grad, right_whole],
        [pltpu.VMEM((2, 8, 2, 16, 1024), F32)],
        flops=2 * flops,
    )
    right_other = (keep[1] + swap(send_other, PAIR).astype(F32)).astype(BF16)
    right_got = swap(send_mine, PAIR)
    (sums,) = call(
        gather_kernel,
        [shape((4, 2, 4, 4, 32, 128), BF16)],
        [place, left_keep, swap(left_send, "c"), keep[0], right_got, swap(right_other, "c")],
    )
    home = to_owners(sums.reshape(128, 32, 128))
    return (home[:, :16] * tile_mask, home[:, 16:] * tile_mask)


def solution(mesh):
    fine = Mesh(mesh.devices.reshape(SIZES), AXES)
    tile = P(None, ROW, COL)
    return jax.shard_map(
        on_device,
        mesh=fine,
        in_specs=(tile, tile, tile, tile, P(), P(), P()),
        out_specs=(tile, tile),
        check_vma=False,
    )
```

```python
import jax
import jax.numpy as jnp
from jax import lax
from jax.experimental import pallas as pl
from jax.experimental.pallas import tpu as pltpu
from jax.sharding import Mesh, PartitionSpec as P

norm_eps = 1e-05

AXES = ("zl", "y", "xh", "xl", "zh", "c")
SIZES = (4, 4, 2, 2, 4, 2)
ROW = ("zl", "y", "xh", "xl")
COL = ("zh", "c")
PAIR = "xh"
OWNERS = ("zl", "y", "xl", "zh")
BF16 = jnp.bfloat16
F32 = jnp.float32
VMEM_LIMIT = 32 * 1024 * 1024


def lanes(z, half=0):
    return slice(512 * half + 128 * z, 512 * half + 128 * (z + 1))


def whole_left(both_ref, left_low_ref, left_high_ref, i_mask_ref, k_mask_ref):
    parts = [both_ref[:, z, 0:16, :].reshape(512, 128) for z in range(4)]
    for z in range(4):
        ends = [ref[:, z, :, :].reshape(256, 128) for ref in (left_low_ref, left_high_ref)]
        parts.append(jnp.concatenate(ends, axis=0))
    i_mask = i_mask_ref[...]
    masks = [i_mask * k_mask_ref[0:1, 128 * n : 128 * (n + 1)] for n in range(8)]
    return jnp.concatenate([part * mask for part, mask in zip(parts, masks)], axis=1)


def whole_grad(grad_ref):
    return jnp.concatenate([grad_ref[:, z, :, :].reshape(512, 128) for z in range(4)], axis=1)


def product_kernel(
    place_ref, i_mask_ref, j_mask_ref, k_mask_ref, both_ref, left_low_ref, left_high_ref, near_ref, far_0_ref, far_1_ref,
    out_ref, right_ref,
):
    pair, core = place_ref[0], place_ref[1]

    j_masks = j_mask_ref[...].reshape(4, 2, 2, 2, 16, 128)

    def place(bit, source):
        mask = jnp.where(bit == 0, j_masks[:, :, 0], j_masks[:, :, 1])
        for z in range(4):
            for half in range(2):
                rows = source[half, :, z, :, :].reshape(4, 2, 2, 16, 128)
                right_ref[:, :, bit, :, :, lanes(z, half)] = rows * mask

    place(pair, near_ref)

    @pl.when(core == 0)
    def _():
        place(1 - pair, far_0_ref)

    @pl.when(core == 1)
    def _():
        place(1 - pair, far_1_ref)

    product = lax.dot_general(
        whole_left(both_ref, left_low_ref, left_high_ref, i_mask_ref, k_mask_ref),
        right_ref[...].reshape(512, 1024),
        (((1,), (1,)), ((), ())),
        preferred_element_type=F32,
    )
    for z in range(4):
        out_ref[:, z, :, :] = product[:, lanes(z)].reshape(32, 16, 128).astype(BF16)


def right_grad_kernel(
    place_ref, i_mask_ref, k_mask_ref, both_ref, left_low_ref, left_high_ref, grad_ref, send_ref, keep_ref
):
    pair = place_ref[0]
    part = lax.dot_general(
        whole_grad(grad_ref),
        whole_left(both_ref, left_low_ref, left_high_ref, i_mask_ref, k_mask_ref),
        (((0,), (0,)), ((), ())),
        preferred_element_type=F32,
    ).reshape(8, 2, 2, 16, 1024)
    send = jnp.where(pair == 0, part[:, 1], part[:, 0]).astype(BF16)
    keep = jnp.where(pair == 0, part[:, 0], part[:, 1])
    for z in range(4):
        for half in range(2):
            cols = lanes(z, half)
            send_ref[half, :, z, :, :] = send[..., cols].reshape(16, 16, 128)
            keep_ref[half, :, z, :, :] = keep[..., cols].reshape(16, 16, 128)


def left_grad_kernel(place_ref, grad_ref, right_ref, send_ref, keep_ref):
    part = jnp.dot(
        whole_grad(grad_ref), right_ref[...].reshape(512, 1024), preferred_element_type=F32
    )
    for z in range(4):
        keep_ref[:, z, :, :] = part[:, lanes(z)].reshape(32, 16, 128)
        send_ref[:, z, :, :] = part[:, lanes(z, 1)].reshape(32, 16, 128).astype(BF16)


def gather_kernel(place_ref, left_keep_ref, left_got_ref, right_keep_ref, right_got_ref, right_other_ref, out_ref):
    core = place_ref[1]
    out_ref[:, :, :, :, 0:16, :] = (
        (left_keep_ref[...] + left_got_ref[...].astype(F32)).astype(BF16).reshape(4, 2, 4, 4, 16, 128)
    )
    out_ref[:, core, :, :, 16:32, :] = (
        (right_keep_ref[0] + right_got_ref[0].astype(F32)).astype(BF16).reshape(4, 4, 4, 16, 128)
    )
    out_ref[:, 1 - core, :, :, 16:32, :] = right_other_ref[...].reshape(4, 4, 4, 16, 128)


def norm_kernel(product_ref, scaled_ref, grad_ref):
    count = product_ref.shape[0]

    def load(c):
        return product_ref[c].astype(F32)

    zeros = jnp.zeros(product_ref.shape[1:], F32)

    def sums(c, carry):
        return carry[0] + load(c), carry[1] + scaled_ref[c]

    total, scaled_total = lax.fori_loop(0, count, sums, (zeros, zeros), unroll=8)
    mean = total * (1.0 / count)
    scaled_mean = scaled_total * (1.0 / count)

    def squares(c, carry):
        center = load(c) - mean
        return carry[0] + center * center, carry[1] + scaled_ref[c] * center

    square, cross = lax.fori_loop(0, count, squares, (zeros, zeros), unroll=8)
    inv_std = lax.rsqrt(square * (1.0 / count) + norm_eps)
    slope = inv_std * inv_std * cross * (1.0 / count)

    def write(c, carry):
        center = load(c) - mean
        grad_ref[c] = (inv_std * (scaled_ref[c] - scaled_mean - center * slope)).astype(BF16)
        return carry

    lax.fori_loop(0, count, write, 0, unroll=8)


def vmem():
    return pl.BlockSpec(memory_space=pltpu.VMEM)


def smem():
    return pl.BlockSpec(memory_space=pltpu.SMEM)


def shape(dims, dtype):
    return jax.ShapeDtypeStruct(dims, dtype)


def call(kernel, outs, operands, scratch=(), flops=0, scalars=1):
    moved = sum(o.size * o.dtype.itemsize for o in (*operands, *outs))
    return pl.pallas_call(
        kernel,
        out_shape=outs,
        in_specs=[smem()] * scalars + [vmem()] * (len(operands) - scalars),
        out_specs=[vmem()] * len(outs),
        scratch_shapes=scratch,
        compiler_params=pltpu.CompilerParams(vmem_limit_bytes=VMEM_LIMIT),
        cost_estimate=pl.CostEstimate(flops=flops, bytes_accessed=moved, transcendentals=0),
    )(*operands)


def swap(x, axis):
    return lax.ppermute(x, axis, [(0, 1), (1, 0)])


def swap_pair(x, core):
    at = [2 * bit + core for bit in range(2)]
    return lax.ppermute(x, (PAIR, "c"), [(at[0], at[1]), (at[1], at[0])])


def to_owners(x):
    return lax.all_to_all(x, OWNERS, split_axis=0, concat_axis=0, tiled=True)


def on_device(left, right, gate_out, out_grad, norm_gain, out_weight, token_mask):
    core = lax.axis_index("c")
    place = jnp.stack([lax.axis_index(PAIR), core]).astype(jnp.int32)
    pair = lax.axis_index(PAIR)
    both = to_owners(jnp.concatenate([left, right], axis=1))

    tokens = token_mask.astype(BF16)
    i_mask = lax.dynamic_index_in_dim(tokens.reshape(16, 2, 32), pair, 1, keepdims=False).reshape(512, 1)
    halves = tokens.reshape(4, 2, 128)
    mine_mask = lax.dynamic_index_in_dim(halves, core, 1, keepdims=False).reshape(512)
    other_mask = lax.dynamic_index_in_dim(halves, 1 - core, 1, keepdims=False).reshape(512)
    i_mask = jnp.broadcast_to(i_mask, (512, 128))
    j_mask = jnp.broadcast_to(mine_mask[:, None], (512, 128))
    k_mask = jnp.broadcast_to(jnp.concatenate([mine_mask, other_mask])[None], (16, 1024))
    row_mask = lax.dynamic_slice_in_dim(tokens, lax.axis_index(ROW) * 16, 16)
    col_mask = lax.dynamic_slice_in_dim(tokens, lax.axis_index(COL) * 128, 128)
    tile_mask = (row_mask[:, None] * col_mask[None, :])[None]
    gated_grad = (gate_out.astype(F32) * out_grad.astype(F32)).astype(BF16)
    linear = jnp.dot(
        out_weight, gated_grad.reshape(gated_grad.shape[0], -1), preferred_element_type=F32
    )
    scaled = norm_gain[:, None, None] * linear.reshape(left.shape)
    both, i_mask, j_mask, k_mask, tile_mask, scaled = lax.optimization_barrier(
        (both, i_mask, j_mask, k_mask, tile_mask, scaled)
    )

    half = (16, 4, 16, 128)
    rows = both.reshape(4, 2, 4, 4, 32, 128)[:, :, :, :, 16:, :]
    mine = lax.dynamic_index_in_dim(rows, core, 1, keepdims=False).reshape(half)
    other = swap(lax.dynamic_index_in_dim(rows, 1 - core, 1, keepdims=False).reshape(half), "c")
    near = jnp.stack([mine, other])
    far_1 = swap_pair(near, 1)
    both = both.reshape(32, 4, 32, 128)
    left_low, left_high, near = lax.optimization_barrier((both[:16, :, :16, :], both[16:, :, :16, :], near))
    left_low, left_high = swap(left_low, "c"), swap(left_high, "c")
    near_0, far_1, left_low, left_high = lax.optimization_barrier((near, far_1, left_low, left_high))
    far_0 = swap_pair(near_0, 0)

    flops = 2 * 512 * 512 * 1024
    blocks = (32, 4, 16, 128)
    product, right_whole = call(
        product_kernel,
        [shape(blocks, BF16), shape((4, 2, 2, 2, 16, 1024), BF16)],
        [place, i_mask, j_mask, k_mask, both, left_low, left_high, near, far_0, far_1],
        flops=flops,
    )
    product = to_owners(product.reshape(left.shape))
    (grad,) = call(
        norm_kernel,
        [shape(left.shape, BF16)],
        [product, scaled],
        flops=20 * product.size,
        scalars=0,
    )
    grad = to_owners(grad).reshape(blocks)

    half = (16, 4, 16, 128)
    right_send, right_keep = call(
        right_grad_kernel,
        [shape((2, *half), BF16), shape((2, *half), F32)],
        [place, i_mask, k_mask, both, left_low, left_high, grad],
        flops=flops,
    )
    right_got = swap(right_send, PAIR)
    right_other = (right_keep[1] + right_got[1].astype(F32)).astype(BF16)
    left_send, left_keep = call(
        left_grad_kernel, [shape(blocks, BF16), shape(blocks, F32)], [place, grad, right_whole], flops=flops
    )
    (sums,) = call(
        gather_kernel,
        [shape((4, 2, 4, 4, 32, 128), BF16)],
        [place, left_keep, swap(left_send, "c"), right_keep, right_got, swap(right_other, "c")],
    )
    home = to_owners(sums.reshape(128, 32, 128))
    return (home[:, :16] * tile_mask, home[:, 16:] * tile_mask)


def solution(mesh):
    fine = Mesh(mesh.devices.reshape(SIZES), AXES)
    tile = P(None, ROW, COL)
    return jax.shard_map(
        on_device,
        mesh=fine,
        in_specs=(tile, tile, tile, tile, P(), P(), P()),
        out_specs=(tile, tile),
        check_vma=False,
    )
```

```python
import jax
import jax.numpy as jnp
from jax import lax
from jax.experimental import pallas as pl
from jax.experimental.pallas import tpu as pltpu
from jax.sharding import Mesh, PartitionSpec as P

norm_eps = 1e-05

AXES = ("zl", "y", "xh", "xl", "zh", "c")
SIZES = (4, 4, 2, 2, 4, 2)
ROW = ("zl", "y", "xh", "xl")
COL = ("zh", "c")
PAIR = "xh"
OWNERS = ("zl", "y", "xl", "zh")
BF16 = jnp.bfloat16
F32 = jnp.float32
VMEM_LIMIT = 32 * 1024 * 1024


def lanes(z, half=0):
    return slice(512 * half + 128 * z, 512 * half + 128 * (z + 1))


def place_rows(bit, halves, j_mask_ref, right_ref):
    j_masks = j_mask_ref[...].reshape(4, 2, 2, 2, 16, 128)
    mask = jnp.where(bit == 0, j_masks[:, :, 0], j_masks[:, :, 1])
    for z in range(4):
        for half in range(2):
            rows = halves[half, :, z, :, :].reshape(4, 2, 2, 16, 128)
            right_ref[:, :, bit, :, :, lanes(z, half)] = rows * mask


def near_kernel(
    place_ref, i_mask_ref, j_mask_ref, k_mask_ref, both_ref, left_low_ref, left_high_ref, near_ref, out_ref, right_ref
):
    parts = [both_ref[:, z, 0:16, :].reshape(512, 128) for z in range(4)]
    for z in range(4):
        ends = [ref[:, z, :, :].reshape(256, 128) for ref in (left_low_ref, left_high_ref)]
        parts.append(jnp.concatenate(ends, axis=0))
    i_mask = i_mask_ref[...]
    for n, part in enumerate(parts):
        cols = slice(128 * n, 128 * (n + 1))
        out_ref[:, cols] = part * (i_mask * k_mask_ref[0:1, cols])
    place_rows(place_ref[0], near_ref, j_mask_ref, right_ref)
    zeros = jnp.zeros((4, 2, 2, 16, 1024), BF16)
    right_ref[:, :, 1 - place_ref[0], :, :, :] = zeros


def whole_grad(grad_ref):
    return jnp.concatenate([grad_ref[:, z, :, :].reshape(512, 128) for z in range(4)], axis=1)


def product_kernel(place_ref, j_mask_ref, left_ref, far_0_ref, far_1_ref, right_in_ref, out_ref, right_ref):
    pair, core = place_ref[0], place_ref[1]
    del right_in_ref

    @pl.when(core == 0)
    def _():
        place_rows(1 - pair, far_0_ref, j_mask_ref, right_ref)

    @pl.when(core == 1)
    def _():
        place_rows(1 - pair, far_1_ref, j_mask_ref, right_ref)

    product = lax.dot_general(
        left_ref[...],
        right_ref[...].reshape(512, 1024),
        (((1,), (1,)), ((), ())),
        preferred_element_type=F32,
    )
    for z in range(4):
        out_ref[:, z, :, :] = product[:, lanes(z)].reshape(32, 16, 128).astype(BF16)


def right_grad_kernel(
    place_ref, left_ref, grad_ref, send_ref, keep_ref
):
    pair = place_ref[0]
    part = lax.dot_general(
        whole_grad(grad_ref),
        left_ref[...],
        (((0,), (0,)), ((), ())),
        preferred_element_type=F32,
    ).reshape(8, 2, 2, 16, 1024)
    send = jnp.where(pair == 0, part[:, 1], part[:, 0]).astype(BF16)
    keep = jnp.where(pair == 0, part[:, 0], part[:, 1])
    for z in range(4):
        for half in range(2):
            cols = lanes(z, half)
            send_ref[half, :, z, :, :] = send[..., cols].reshape(16, 16, 128)
            keep_ref[half, :, z, :, :] = keep[..., cols].reshape(16, 16, 128)


def left_grad_kernel(place_ref, grad_ref, right_ref, send_ref, keep_ref):
    part = jnp.dot(
        whole_grad(grad_ref), right_ref[...].reshape(512, 1024), preferred_element_type=F32
    )
    for z in range(4):
        keep_ref[:, z, :, :] = part[:, lanes(z)].reshape(32, 16, 128)
        send_ref[:, z, :, :] = part[:, lanes(z, 1)].reshape(32, 16, 128).astype(BF16)


def gather_kernel(place_ref, left_keep_ref, left_got_ref, right_keep_ref, right_got_ref, out_ref):
    core = place_ref[1]
    out_ref[:, :, :, :, 0:16, :] = (
        (left_keep_ref[...] + left_got_ref[...].astype(F32)).astype(BF16).reshape(4, 2, 4, 4, 16, 128)
    )
    right = (right_keep_ref[0] + right_got_ref[0].astype(F32)).astype(BF16).reshape(4, 4, 4, 16, 128)
    out_ref[:, core, :, :, 16:32, :] = right


def norm_kernel(product_ref, scaled_ref, grad_ref):
    count = product_ref.shape[0]

    def load(c):
        return product_ref[c].astype(F32)

    zeros = jnp.zeros(product_ref.shape[1:], F32)

    def sums(c, carry):
        return carry[0] + load(c), carry[1] + scaled_ref[c]

    total, scaled_total = lax.fori_loop(0, count, sums, (zeros, zeros), unroll=8)
    mean = total * (1.0 / count)
    scaled_mean = scaled_total * (1.0 / count)

    def squares(c, carry):
        center = load(c) - mean
        return carry[0] + center * center, carry[1] + scaled_ref[c] * center

    square, cross = lax.fori_loop(0, count, squares, (zeros, zeros), unroll=8)
    inv_std = lax.rsqrt(square * (1.0 / count) + norm_eps)
    slope = inv_std * inv_std * cross * (1.0 / count)

    def write(c, carry):
        center = load(c) - mean
        grad_ref[c] = (inv_std * (scaled_ref[c] - scaled_mean - center * slope)).astype(BF16)
        return carry

    lax.fori_loop(0, count, write, 0, unroll=8)


def vmem():
    return pl.BlockSpec(memory_space=pltpu.VMEM)


def smem():
    return pl.BlockSpec(memory_space=pltpu.SMEM)


def shape(dims, dtype):
    return jax.ShapeDtypeStruct(dims, dtype)


def call(kernel, outs, operands, scratch=(), flops=0, scalars=1, aliases=None):
    moved = sum(o.size * o.dtype.itemsize for o in (*operands, *outs))
    return pl.pallas_call(
        kernel,
        out_shape=outs,
        in_specs=[smem()] * scalars + [vmem()] * (len(operands) - scalars),
        out_specs=[vmem()] * len(outs),
        scratch_shapes=scratch,
        input_output_aliases=aliases or {},
        compiler_params=pltpu.CompilerParams(vmem_limit_bytes=VMEM_LIMIT),
        cost_estimate=pl.CostEstimate(flops=flops, bytes_accessed=moved, transcendentals=0),
    )(*operands)


def swap(x, axis):
    return lax.ppermute(x, axis, [(0, 1), (1, 0)])


def swap_pair(x, core):
    at = [2 * bit + core for bit in range(2)]
    return lax.ppermute(x, (PAIR, "c"), [(at[0], at[1]), (at[1], at[0])])


def to_owners(x):
    return lax.all_to_all(x, OWNERS, split_axis=0, concat_axis=0, tiled=True)


def on_device(left, right, gate_out, out_grad, norm_gain, out_weight, token_mask):
    core = lax.axis_index("c")
    place = jnp.stack([lax.axis_index(PAIR), core]).astype(jnp.int32)
    pair = lax.axis_index(PAIR)
    both = to_owners(jnp.concatenate([left, right], axis=1))

    tokens = token_mask.astype(BF16)
    i_mask = lax.dynamic_index_in_dim(tokens.reshape(16, 2, 32), pair, 1, keepdims=False).reshape(512, 1)
    halves = tokens.reshape(4, 2, 128)
    mine_mask = lax.dynamic_index_in_dim(halves, core, 1, keepdims=False).reshape(512)
    other_mask = lax.dynamic_index_in_dim(halves, 1 - core, 1, keepdims=False).reshape(512)
    i_mask = jnp.broadcast_to(i_mask, (512, 128))
    j_mask = jnp.broadcast_to(mine_mask[:, None], (512, 128))
    k_mask = jnp.broadcast_to(jnp.concatenate([mine_mask, other_mask])[None], (16, 1024))
    row_mask = lax.dynamic_slice_in_dim(tokens, lax.axis_index(ROW) * 16, 16)
    col_mask = lax.dynamic_slice_in_dim(tokens, lax.axis_index(COL) * 128, 128)
    tile_mask = (row_mask[:, None] * col_mask[None, :])[None]
    gated_grad = (gate_out.astype(F32) * out_grad.astype(F32)).astype(BF16)
    linear = jnp.dot(
        out_weight, gated_grad.reshape(gated_grad.shape[0], -1), preferred_element_type=F32
    )
    scaled = norm_gain[:, None, None] * linear.reshape(left.shape)
    both, i_mask, j_mask, k_mask, tile_mask, scaled = lax.optimization_barrier(
        (both, i_mask, j_mask, k_mask, tile_mask, scaled)
    )

    half = (16, 4, 16, 128)
    rows = both.reshape(4, 2, 4, 4, 32, 128)[:, :, :, :, 16:, :]
    mine = lax.dynamic_index_in_dim(rows, core, 1, keepdims=False).reshape(half)
    other = swap(lax.dynamic_index_in_dim(rows, 1 - core, 1, keepdims=False).reshape(half), "c")
    near = jnp.stack([mine, other])
    far_1 = swap_pair(near, 1)
    both = both.reshape(32, 4, 32, 128)
    left_low, left_high, near = lax.optimization_barrier((both[:16, :, :16, :], both[16:, :, :16, :], near))
    left_low, left_high = swap(left_low, "c"), swap(left_high, "c")
    left_whole, right_near = call(
        near_kernel,
        [shape((512, 1024), BF16), shape((4, 2, 2, 2, 16, 1024), BF16)],
        [place, i_mask, j_mask, k_mask, both, left_low, left_high, near],
    )
    near_0, far_1, left_whole, right_near = lax.optimization_barrier((near, far_1, left_whole, right_near))
    far_0 = swap_pair(near_0, 0)

    flops = 2 * 512 * 512 * 1024
    blocks = (32, 4, 16, 128)
    product, right_whole = call(
        product_kernel,
        [shape(blocks, BF16), shape((4, 2, 2, 2, 16, 1024), BF16)],
        [place, j_mask, left_whole, far_0, far_1, right_near],
        aliases={5: 1},
        flops=flops,
    )
    product = to_owners(product.reshape(left.shape))
    (grad,) = call(
        norm_kernel,
        [shape(left.shape, BF16)],
        [product, scaled],
        flops=20 * product.size,
        scalars=0,
    )
    grad = to_owners(grad).reshape(blocks)

    half = (16, 4, 16, 128)
    right_send, right_keep = call(
        right_grad_kernel,
        [shape((2, *half), BF16), shape((2, *half), F32)],
        [place, left_whole, grad],
        flops=flops,
    )
    right_got = swap(right_send, PAIR)
    right_other = (right_keep[1] + right_got[1].astype(F32)).astype(BF16)
    left_send, left_keep = call(
        left_grad_kernel, [shape(blocks, BF16), shape(blocks, F32)], [place, grad, right_whole], flops=flops
    )
    right_other = swap(right_other, "c").reshape(4, 1, 4, 4, 16, 128)
    (sums,) = call(
        gather_kernel,
        [shape((4, 2, 4, 4, 32, 128), BF16)],
        [place, left_keep, swap(left_send, "c"), right_keep, right_got],
    )
    sums = lax.dynamic_update_slice(sums, right_other, (0, 1 - core, 0, 0, 16, 0))
    home = to_owners(sums.reshape(128, 32, 128))
    return (home[:, :16] * tile_mask, home[:, 16:] * tile_mask)


def solution(mesh):
    fine = Mesh(mesh.devices.reshape(SIZES), AXES)
    tile = P(None, ROW, COL)
    return jax.shard_map(
        on_device,
        mesh=fine,
        in_specs=(tile, tile, tile, tile, P(), P(), P()),
        out_specs=(tile, tile),
        check_vma=False,
    )
```

```python
import jax
import jax.numpy as jnp
from jax import lax
from jax.experimental import pallas as pl
from jax.experimental.pallas import tpu as pltpu
from jax.sharding import Mesh, PartitionSpec as P

norm_eps = 1e-05

AXES = ("zl", "y", "xh", "xl", "zh", "c")
SIZES = (4, 4, 2, 2, 4, 2)
ROW = ("zl", "y", "xh", "xl")
COL = ("zh", "c")
PAIR = "xh"
OWNERS = ("zl", "y", "xl", "zh")
BF16 = jnp.bfloat16
F32 = jnp.float32
VMEM_LIMIT = 32 * 1024 * 1024


def lanes(z, half=0):
    return slice(512 * half + 128 * z, 512 * half + 128 * (z + 1))


def place_rows(bit, halves, j_mask_ref, right_ref):
    j_masks = j_mask_ref[...].reshape(4, 2, 2, 2, 16, 128)
    mask = jnp.where(bit == 0, j_masks[:, :, 0], j_masks[:, :, 1])
    for z in range(4):
        for half in range(2):
            rows = halves[half, :, z, :, :].reshape(4, 2, 2, 16, 128)
            right_ref[:, :, bit, :, :, lanes(z, half)] = rows * mask


def near_kernel(
    place_ref, i_mask_ref, j_mask_ref, k_mask_ref, both_ref, left_low_ref, left_high_ref, near_ref, out_ref, right_ref
):
    parts = [both_ref[:, z, 0:16, :].reshape(512, 128) for z in range(4)]
    for z in range(4):
        ends = [ref[:, z, :, :].reshape(256, 128) for ref in (left_low_ref, left_high_ref)]
        parts.append(jnp.concatenate(ends, axis=0))
    i_mask = i_mask_ref[...].reshape(32, 16, 128)
    for n, part in enumerate(parts):
        cols = slice(128 * n, 128 * (n + 1))
        mask = (i_mask * k_mask_ref[:, cols][None]).reshape(512, 128)
        out_ref[:, cols] = part * mask
    place_rows(place_ref[0], near_ref, j_mask_ref, right_ref)
    zeros = jnp.zeros((4, 2, 2, 16, 1024), BF16)
    right_ref[:, :, 1 - place_ref[0], :, :, :] = zeros


def whole_grad(grad_ref):
    return jnp.concatenate([grad_ref[:, z, :, :].reshape(512, 128) for z in range(4)], axis=1)


def product_kernel(place_ref, j_mask_ref, left_ref, far_0_ref, far_1_ref, right_in_ref, out_ref, right_ref):
    pair, core = place_ref[0], place_ref[1]
    del right_in_ref

    @pl.when(core == 0)
    def _():
        place_rows(1 - pair, far_0_ref, j_mask_ref, right_ref)

    @pl.when(core == 1)
    def _():
        place_rows(1 - pair, far_1_ref, j_mask_ref, right_ref)

    product = lax.dot_general(
        left_ref[...],
        right_ref[...].reshape(512, 1024),
        (((1,), (1,)), ((), ())),
        preferred_element_type=F32,
    )
    for z in range(4):
        out_ref[:, z, :, :] = product[:, lanes(z)].reshape(32, 16, 128).astype(BF16)


def right_grad_kernel(
    place_ref, left_ref, grad_ref, send_ref, keep_ref
):
    pair = place_ref[0]
    part = lax.dot_general(
        whole_grad(grad_ref),
        left_ref[...],
        (((0,), (0,)), ((), ())),
        preferred_element_type=F32,
    ).reshape(8, 2, 2, 16, 1024)
    send = jnp.where(pair == 0, part[:, 1], part[:, 0]).astype(BF16)
    keep = jnp.where(pair == 0, part[:, 0], part[:, 1])
    for z in range(4):
        for half in range(2):
            cols = lanes(z, half)
            send_ref[half, :, z, :, :] = send[..., cols].reshape(16, 16, 128)
            keep_ref[half, :, z, :, :] = keep[..., cols].reshape(16, 16, 128)


def left_grad_kernel(place_ref, grad_ref, right_ref, send_ref, keep_ref):
    part = jnp.dot(
        whole_grad(grad_ref), right_ref[...].reshape(512, 1024), preferred_element_type=F32
    )
    for z in range(4):
        keep_ref[:, z, :, :] = part[:, lanes(z)].reshape(32, 16, 128)
        send_ref[:, z, :, :] = part[:, lanes(z, 1)].reshape(32, 16, 128).astype(BF16)


def gather_kernel(place_ref, left_keep_ref, left_got_ref, right_keep_ref, right_got_ref, out_ref):
    core = place_ref[1]
    out_ref[:, :, :, :, 0:16, :] = (
        (left_keep_ref[...] + left_got_ref[...].astype(F32)).astype(BF16).reshape(4, 2, 4, 4, 16, 128)
    )
    right = (right_keep_ref[0] + right_got_ref[0].astype(F32)).astype(BF16).reshape(4, 4, 4, 16, 128)
    out_ref[:, core, :, :, 16:32, :] = right


def norm_kernel(product_ref, scaled_ref, grad_ref):
    count = product_ref.shape[0]

    def load(c):
        return product_ref[c].astype(F32)

    zeros = jnp.zeros(product_ref.shape[1:], F32)

    def sums(c, carry):
        return carry[0] + load(c), carry[1] + scaled_ref[c]

    total, scaled_total = lax.fori_loop(0, count, sums, (zeros, zeros), unroll=8)
    mean = total * (1.0 / count)
    scaled_mean = scaled_total * (1.0 / count)

    def squares(c, carry):
        center = load(c) - mean
        return carry[0] + center * center, carry[1] + scaled_ref[c] * center

    square, cross = lax.fori_loop(0, count, squares, (zeros, zeros), unroll=8)
    inv_std = lax.rsqrt(square * (1.0 / count) + norm_eps)
    slope = inv_std * inv_std * cross * (1.0 / count)

    def write(c, carry):
        center = load(c) - mean
        grad_ref[c] = (inv_std * (scaled_ref[c] - scaled_mean - center * slope)).astype(BF16)
        return carry

    lax.fori_loop(0, count, write, 0, unroll=8)


def vmem():
    return pl.BlockSpec(memory_space=pltpu.VMEM)


def smem():
    return pl.BlockSpec(memory_space=pltpu.SMEM)


def shape(dims, dtype):
    return jax.ShapeDtypeStruct(dims, dtype)


def call(kernel, outs, operands, scratch=(), flops=0, scalars=1, aliases=None):
    moved = sum(o.size * o.dtype.itemsize for o in (*operands, *outs))
    return pl.pallas_call(
        kernel,
        out_shape=outs,
        in_specs=[smem()] * scalars + [vmem()] * (len(operands) - scalars),
        out_specs=[vmem()] * len(outs),
        scratch_shapes=scratch,
        input_output_aliases=aliases or {},
        compiler_params=pltpu.CompilerParams(vmem_limit_bytes=VMEM_LIMIT),
        cost_estimate=pl.CostEstimate(flops=flops, bytes_accessed=moved, transcendentals=0),
    )(*operands)


def swap(x, axis):
    return lax.ppermute(x, axis, [(0, 1), (1, 0)])


def swap_pair(x, core):
    at = [2 * bit + core for bit in range(2)]
    return lax.ppermute(x, (PAIR, "c"), [(at[0], at[1]), (at[1], at[0])])


def to_owners(x):
    return lax.all_to_all(x, OWNERS, split_axis=0, concat_axis=0, tiled=True)


def on_device(left, right, gate_out, out_grad, norm_gain, out_weight, token_mask):
    core = lax.axis_index("c")
    place = jnp.stack([lax.axis_index(PAIR), core]).astype(jnp.int32)
    pair = lax.axis_index(PAIR)
    both = to_owners(jnp.concatenate([left, right], axis=1))

    tokens = token_mask.astype(BF16)
    i_mask = lax.dynamic_index_in_dim(tokens.reshape(16, 2, 32), pair, 1, keepdims=False).reshape(512, 1)
    halves = tokens.reshape(4, 2, 128)
    mine_mask = lax.dynamic_index_in_dim(halves, core, 1, keepdims=False).reshape(512)
    other_mask = lax.dynamic_index_in_dim(halves, 1 - core, 1, keepdims=False).reshape(512)
    i_mask = jnp.broadcast_to(i_mask, (512, 128))
    j_mask = jnp.broadcast_to(mine_mask[:, None], (512, 128))
    k_mask = jnp.broadcast_to(jnp.concatenate([mine_mask, other_mask])[None], (16, 1024))
    row_mask = lax.dynamic_slice_in_dim(tokens, lax.axis_index(ROW) * 16, 16)
    col_mask = lax.dynamic_slice_in_dim(tokens, lax.axis_index(COL) * 128, 128)
    tile_mask = (row_mask[:, None] * col_mask[None, :])[None]
    gated_grad = (gate_out.astype(F32) * out_grad.astype(F32)).astype(BF16)
    linear = jnp.dot(
        out_weight, gated_grad.reshape(gated_grad.shape[0], -1), preferred_element_type=F32
    )
    scaled = norm_gain[:, None, None] * linear.reshape(left.shape)
    both, i_mask, j_mask, k_mask, tile_mask, scaled = lax.optimization_barrier(
        (both, i_mask, j_mask, k_mask, tile_mask, scaled)
    )

    half = (16, 4, 16, 128)
    rows = both.reshape(4, 2, 4, 4, 32, 128)[:, :, :, :, 16:, :]
    mine = lax.dynamic_index_in_dim(rows, core, 1, keepdims=False).reshape(half)
    other = swap(lax.dynamic_index_in_dim(rows, 1 - core, 1, keepdims=False).reshape(half), "c")
    near = jnp.stack([mine, other])
    far_1 = swap_pair(near, 1)
    both = both.reshape(32, 4, 32, 128)
    left_low, left_high, near = lax.optimization_barrier((both[:16, :, :16, :], both[16:, :, :16, :], near))
    left_low, left_high = swap(left_low, "c"), swap(left_high, "c")
    left_whole, right_near = call(
        near_kernel,
        [shape((512, 1024), BF16), shape((4, 2, 2, 2, 16, 1024), BF16)],
        [place, i_mask, j_mask, k_mask, both, left_low, left_high, near],
    )
    near_0, far_1, left_whole, right_near = lax.optimization_barrier((near, far_1, left_whole, right_near))
    far_0 = swap_pair(near_0, 0)

    flops = 2 * 512 * 512 * 1024
    blocks = (32, 4, 16, 128)
    product, right_whole = call(
        product_kernel,
        [shape(blocks, BF16), shape((4, 2, 2, 2, 16, 1024), BF16)],
        [place, j_mask, left_whole, far_0, far_1, right_near],
        aliases={5: 1},
        flops=flops,
    )
    product = to_owners(product.reshape(left.shape))
    (grad,) = call(
        norm_kernel,
        [shape(left.shape, BF16)],
        [product, scaled],
        flops=20 * product.size,
        scalars=0,
    )
    grad = to_owners(grad).reshape(blocks)

    half = (16, 4, 16, 128)
    right_send, right_keep = call(
        right_grad_kernel,
        [shape((2, *half), BF16), shape((2, *half), F32)],
        [place, left_whole, grad],
        flops=flops,
    )
    right_got = swap(right_send, PAIR)
    right_other = (right_keep[1] + right_got[1].astype(F32)).astype(BF16)
    left_send, left_keep = call(
        left_grad_kernel, [shape(blocks, BF16), shape(blocks, F32)], [place, grad, right_whole], flops=flops
    )
    right_other = swap(right_other, "c").reshape(4, 1, 4, 4, 16, 128)
    (sums,) = call(
        gather_kernel,
        [shape((4, 2, 4, 4, 32, 128), BF16)],
        [place, left_keep, swap(left_send, "c"), right_keep, right_got],
    )
    sums = lax.dynamic_update_slice(sums, right_other, (0, 1 - core, 0, 0, 16, 0))
    home = to_owners(sums.reshape(128, 32, 128))
    return (home[:, :16] * tile_mask, home[:, 16:] * tile_mask)


def solution(mesh):
    fine = Mesh(mesh.devices.reshape(SIZES), AXES)
    tile = P(None, ROW, COL)
    return jax.shard_map(
        on_device,
        mesh=fine,
        in_specs=(tile, tile, tile, tile, P(), P(), P()),
        out_specs=(tile, tile),
        check_vma=False,
    )
```

```python
import jax
import jax.numpy as jnp
from jax import lax
from jax.experimental import pallas as pl
from jax.experimental.pallas import tpu as pltpu
from jax.sharding import Mesh, PartitionSpec as P

norm_eps = 1e-05

AXES = ("zl", "y", "xh", "xl", "zh", "c")
SIZES = (4, 4, 2, 2, 4, 2)
ROW = ("zl", "y", "xh", "xl")
COL = ("zh", "c")
PAIR = "xh"
OWNERS = ("zl", "y", "xl", "zh")
BF16 = jnp.bfloat16
F32 = jnp.float32
VMEM_LIMIT = 32 * 1024 * 1024


def lanes(z, half=0):
    return slice(512 * half + 128 * z, 512 * half + 128 * (z + 1))


def place_rows(bit, halves, j_mask_ref, right_ref):
    j_masks = j_mask_ref[...].reshape(4, 2, 2, 2, 16, 128)
    mask = jnp.where(bit == 0, j_masks[:, :, 0], j_masks[:, :, 1])
    for z in range(4):
        for half in range(2):
            rows = halves[half, :, z, :, :].reshape(4, 2, 2, 16, 128)
            right_ref[:, :, bit, :, :, lanes(z, half)] = rows * mask


def near_kernel(
    place_ref, i_mask_ref, j_mask_ref, k_mask_ref, both_ref, left_low_ref, left_high_ref, near_ref, out_ref, right_ref
):
    parts = [both_ref[:, z, 0:16, :].reshape(512, 128) for z in range(4)]
    for z in range(4):
        ends = [ref[:, z, :, :].reshape(256, 128) for ref in (left_low_ref, left_high_ref)]
        parts.append(jnp.concatenate(ends, axis=0))
    i_mask = i_mask_ref[...].reshape(32, 16, 128)
    for n, part in enumerate(parts):
        cols = slice(128 * n, 128 * (n + 1))
        mask = (i_mask * k_mask_ref[:, cols][None]).reshape(512, 128)
        out_ref[:, cols] = part * mask
    place_rows(place_ref[0], near_ref, j_mask_ref, right_ref)
    zeros = jnp.zeros((4, 2, 2, 16, 1024), BF16)
    right_ref[:, :, 1 - place_ref[0], :, :, :] = zeros


def whole_grad(grad_ref):
    return jnp.concatenate([grad_ref[:, z, :, :].reshape(512, 128) for z in range(4)], axis=1)


def product_kernel(place_ref, j_mask_ref, left_ref, far_0_ref, far_1_ref, right_in_ref, out_ref, right_ref):
    pair, core = place_ref[0], place_ref[1]
    del right_in_ref

    @pl.when(core == 0)
    def _():
        place_rows(1 - pair, far_0_ref, j_mask_ref, right_ref)

    @pl.when(core == 1)
    def _():
        place_rows(1 - pair, far_1_ref, j_mask_ref, right_ref)

    product = lax.dot_general(
        left_ref[...],
        right_ref[...].reshape(512, 1024),
        (((1,), (1,)), ((), ())),
        preferred_element_type=F32,
    )
    for z in range(4):
        out_ref[:, z, :, :] = product[:, lanes(z)].reshape(32, 16, 128).astype(BF16)


def right_grad_kernel(
    place_ref, left_ref, grad_ref, send_ref, keep_ref
):
    pair = place_ref[0]
    part = lax.dot_general(
        whole_grad(grad_ref),
        left_ref[...],
        (((0,), (0,)), ((), ())),
        preferred_element_type=F32,
    ).reshape(8, 2, 2, 16, 1024)
    send = jnp.where(pair == 0, part[:, 1], part[:, 0]).astype(BF16)
    keep = jnp.where(pair == 0, part[:, 0], part[:, 1])
    for z in range(4):
        for half in range(2):
            cols = lanes(z, half)
            send_ref[half, :, z, :, :] = send[..., cols].reshape(16, 16, 128)
            keep_ref[half, :, z, :, :] = keep[..., cols].reshape(16, 16, 128)


def left_grad_kernel(place_ref, grad_ref, right_ref, send_ref, keep_ref):
    part = jnp.dot(
        whole_grad(grad_ref), right_ref[...].reshape(512, 1024), preferred_element_type=F32
    )
    for z in range(4):
        keep_ref[:, z, :, :] = part[:, lanes(z)].reshape(32, 16, 128)
        send_ref[:, z, :, :] = part[:, lanes(z, 1)].reshape(32, 16, 128).astype(BF16)


def norm_kernel(product_ref, scaled_ref, grad_ref):
    count = product_ref.shape[0]

    def load(c):
        return product_ref[c].astype(F32)

    zeros = jnp.zeros(product_ref.shape[1:], F32)

    def sums(c, carry):
        return carry[0] + load(c), carry[1] + scaled_ref[c]

    total, scaled_total = lax.fori_loop(0, count, sums, (zeros, zeros), unroll=8)
    mean = total * (1.0 / count)
    scaled_mean = scaled_total * (1.0 / count)

    def squares(c, carry):
        center = load(c) - mean
        return carry[0] + center * center, carry[1] + scaled_ref[c] * center

    square, cross = lax.fori_loop(0, count, squares, (zeros, zeros), unroll=8)
    inv_std = lax.rsqrt(square * (1.0 / count) + norm_eps)
    slope = inv_std * inv_std * cross * (1.0 / count)

    def write(c, carry):
        center = load(c) - mean
        grad_ref[c] = (inv_std * (scaled_ref[c] - scaled_mean - center * slope)).astype(BF16)
        return carry

    lax.fori_loop(0, count, write, 0, unroll=8)


def vmem():
    return pl.BlockSpec(memory_space=pltpu.VMEM)


def smem():
    return pl.BlockSpec(memory_space=pltpu.SMEM)


def shape(dims, dtype):
    return jax.ShapeDtypeStruct(dims, dtype)


def call(kernel, outs, operands, scratch=(), flops=0, scalars=1, aliases=None):
    moved = sum(o.size * o.dtype.itemsize for o in (*operands, *outs))
    return pl.pallas_call(
        kernel,
        out_shape=outs,
        in_specs=[smem()] * scalars + [vmem()] * (len(operands) - scalars),
        out_specs=[vmem()] * len(outs),
        scratch_shapes=scratch,
        input_output_aliases=aliases or {},
        compiler_params=pltpu.CompilerParams(vmem_limit_bytes=VMEM_LIMIT),
        cost_estimate=pl.CostEstimate(flops=flops, bytes_accessed=moved, transcendentals=0),
    )(*operands)


def swap(x, axis):
    return lax.ppermute(x, axis, [(0, 1), (1, 0)])


def swap_pair(x, core):
    at = [2 * bit + core for bit in range(2)]
    return lax.ppermute(x, (PAIR, "c"), [(at[0], at[1]), (at[1], at[0])])


def to_owners(x):
    return lax.all_to_all(x, OWNERS, split_axis=0, concat_axis=0, tiled=True)


def on_device(left, right, gate_out, out_grad, norm_gain, out_weight, token_mask):
    core = lax.axis_index("c")
    place = jnp.stack([lax.axis_index(PAIR), core]).astype(jnp.int32)
    pair = lax.axis_index(PAIR)
    both = to_owners(jnp.concatenate([left, right], axis=1))

    tokens = token_mask.astype(BF16)
    i_mask = lax.dynamic_index_in_dim(tokens.reshape(16, 2, 32), pair, 1, keepdims=False).reshape(512, 1)
    halves = tokens.reshape(4, 2, 128)
    mine_mask = lax.dynamic_index_in_dim(halves, core, 1, keepdims=False).reshape(512)
    other_mask = lax.dynamic_index_in_dim(halves, 1 - core, 1, keepdims=False).reshape(512)
    i_mask = jnp.broadcast_to(i_mask, (512, 128))
    j_mask = jnp.broadcast_to(mine_mask[:, None], (512, 128))
    k_mask = jnp.broadcast_to(jnp.concatenate([mine_mask, other_mask])[None], (16, 1024))
    row_mask = lax.dynamic_slice_in_dim(tokens, lax.axis_index(ROW) * 16, 16)
    col_mask = lax.dynamic_slice_in_dim(tokens, lax.axis_index(COL) * 128, 128)
    tile_mask = (row_mask[:, None] * col_mask[None, :])[None]
    gated_grad = (gate_out.astype(F32) * out_grad.astype(F32)).astype(BF16)
    linear = jnp.dot(
        out_weight, gated_grad.reshape(gated_grad.shape[0], -1), preferred_element_type=F32
    )
    scaled = norm_gain[:, None, None] * linear.reshape(left.shape)
    both, i_mask, j_mask, k_mask, tile_mask, scaled = lax.optimization_barrier(
        (both, i_mask, j_mask, k_mask, tile_mask, scaled)
    )

    half = (16, 4, 16, 128)
    rows = both.reshape(4, 2, 4, 4, 32, 128)[:, :, :, :, 16:, :]
    mine = lax.dynamic_index_in_dim(rows, core, 1, keepdims=False).reshape(half)
    other = swap(lax.dynamic_index_in_dim(rows, 1 - core, 1, keepdims=False).reshape(half), "c")
    near = jnp.stack([mine, other])
    far_1 = swap_pair(near, 1)
    both = both.reshape(32, 4, 32, 128)
    left_low, left_high, near = lax.optimization_barrier((both[:16, :, :16, :], both[16:, :, :16, :], near))
    left_low, left_high = swap(left_low, "c"), swap(left_high, "c")
    left_whole, right_near = call(
        near_kernel,
        [shape((512, 1024), BF16), shape((4, 2, 2, 2, 16, 1024), BF16)],
        [place, i_mask, j_mask, k_mask, both, left_low, left_high, near],
    )
    near_0, far_1, left_whole, right_near = lax.optimization_barrier((near, far_1, left_whole, right_near))
    far_0 = swap_pair(near_0, 0)

    flops = 2 * 512 * 512 * 1024
    blocks = (32, 4, 16, 128)
    product, right_whole = call(
        product_kernel,
        [shape(blocks, BF16), shape((4, 2, 2, 2, 16, 1024), BF16)],
        [place, j_mask, left_whole, far_0, far_1, right_near],
        aliases={5: 1},
        flops=flops,
    )
    product = to_owners(product.reshape(left.shape))
    (grad,) = call(
        norm_kernel,
        [shape(left.shape, BF16)],
        [product, scaled],
        flops=20 * product.size,
        scalars=0,
    )
    grad = to_owners(grad).reshape(blocks)

    half = (16, 4, 16, 128)
    right_send, right_keep = call(
        right_grad_kernel,
        [shape((2, *half), BF16), shape((2, *half), F32)],
        [place, left_whole, grad],
        flops=flops,
    )
    got_1 = swap_pair(right_send, 1)
    left_send, left_keep = call(
        left_grad_kernel, [shape(blocks, BF16), shape(blocks, F32)], [place, grad, right_whole], flops=flops
    )
    left_got = swap(left_send, "c")
    right_send, got_1 = lax.optimization_barrier((right_send, got_1))
    got_0 = swap_pair(right_send, 0)
    left_sum = (left_keep + left_got.astype(F32)).astype(BF16)
    left_sum, got_0 = lax.optimization_barrier((left_sum, got_0))
    left_home = to_owners(left_sum.reshape(left.shape))
    total = (right_keep + got_1.astype(F32) + got_0.astype(F32)).astype(BF16).reshape(2, 4, 4, 4, 16, 128)
    across = swap(total[1], "c")
    right_sum = jnp.where(
        core == 0, jnp.stack([total[0], across], axis=1), jnp.stack([across, total[0]], axis=1)
    )
    right_home = to_owners(right_sum.reshape(left.shape))
    return (left_home * tile_mask, right_home * tile_mask)


def solution(mesh):
    fine = Mesh(mesh.devices.reshape(SIZES), AXES)
    tile = P(None, ROW, COL)
    return jax.shard_map(
        on_device,
        mesh=fine,
        in_specs=(tile, tile, tile, tile, P(), P(), P()),
        out_specs=(tile, tile),
        check_vma=False,
    )
```

```python
import jax
import jax.numpy as jnp
from jax import lax
from jax.experimental import pallas as pl
from jax.experimental.pallas import tpu as pltpu
from jax.sharding import Mesh, PartitionSpec as P

norm_eps = 1e-05

AXES = ("zl", "y", "xh", "xl", "zh", "c")
SIZES = (4, 4, 2, 2, 4, 2)
ROW = ("zl", "y", "xh", "xl")
COL = ("zh", "c")
PAIR = "xh"
OWNERS = ("zl", "y", "xl", "zh")
BF16 = jnp.bfloat16
F32 = jnp.float32
VMEM_LIMIT = 32 * 1024 * 1024


def lanes(z, half=0):
    return slice(512 * half + 128 * z, 512 * half + 128 * (z + 1))


def place_rows(bit, halves, j_mask_ref, right_ref):
    j_masks = j_mask_ref[...].reshape(4, 2, 2, 2, 16, 128)
    mask = jnp.where(bit == 0, j_masks[:, :, 0], j_masks[:, :, 1])
    for z in range(4):
        for half in range(2):
            rows = halves[half, :, z, :, :].reshape(4, 2, 2, 16, 128)
            right_ref[:, :, bit, :, :, lanes(z, half)] = rows * mask


def near_kernel(
    place_ref, i_mask_ref, j_mask_ref, k_mask_ref, both_ref, left_low_ref, left_high_ref, near_ref, out_ref, right_ref
):
    parts = [both_ref[:, z, 0:16, :].reshape(512, 128) for z in range(4)]
    for z in range(4):
        ends = [ref[:, z, :, :].reshape(256, 128) for ref in (left_low_ref, left_high_ref)]
        parts.append(jnp.concatenate(ends, axis=0))
    i_mask = i_mask_ref[...].reshape(32, 16, 128)
    for n, part in enumerate(parts):
        cols = slice(128 * n, 128 * (n + 1))
        mask = (i_mask * k_mask_ref[:, cols][None]).reshape(512, 128)
        out_ref[:, cols] = part * mask
    place_rows(place_ref[0], near_ref, j_mask_ref, right_ref)
    zeros = jnp.zeros((4, 2, 2, 16, 1024), BF16)
    right_ref[:, :, 1 - place_ref[0], :, :, :] = zeros


def whole_grad(grad_ref):
    return jnp.concatenate([grad_ref[:, z, :, :].reshape(512, 128) for z in range(4)], axis=1)


def product_kernel(place_ref, j_mask_ref, left_ref, far_0_ref, far_1_ref, right_in_ref, out_ref, right_ref):
    pair, core = place_ref[0], place_ref[1]
    del right_in_ref

    @pl.when(core == 0)
    def _():
        place_rows(1 - pair, far_0_ref, j_mask_ref, right_ref)

    @pl.when(core == 1)
    def _():
        place_rows(1 - pair, far_1_ref, j_mask_ref, right_ref)

    product = lax.dot_general(
        left_ref[...],
        right_ref[...].reshape(512, 1024),
        (((1,), (1,)), ((), ())),
        preferred_element_type=F32,
    )
    for z in range(4):
        out_ref[:, z, :, :] = product[:, lanes(z)].reshape(32, 16, 128).astype(BF16)


def right_grad_kernel(
    place_ref, left_ref, grad_ref, send_ref, keep_ref
):
    pair = place_ref[0]
    part = lax.dot_general(
        whole_grad(grad_ref),
        left_ref[...],
        (((0,), (0,)), ((), ())),
        preferred_element_type=F32,
    ).reshape(8, 2, 2, 16, 1024)
    send = jnp.where(pair == 0, part[:, 1], part[:, 0]).astype(BF16)
    keep = jnp.where(pair == 0, part[:, 0], part[:, 1])
    for z in range(4):
        for half in range(2):
            cols = lanes(z, half)
            send_ref[half, :, z, :, :] = send[..., cols].reshape(16, 16, 128)
            keep_ref[half, :, z, :, :] = keep[..., cols].reshape(16, 16, 128)


def left_grad_kernel(place_ref, grad_ref, right_ref, send_ref, keep_ref):
    part = jnp.dot(
        whole_grad(grad_ref), right_ref[...].reshape(512, 1024), preferred_element_type=F32
    )
    for z in range(4):
        keep_ref[:, z, :, :] = part[:, lanes(z)].reshape(32, 16, 128)
        send_ref[:, z, :, :] = part[:, lanes(z, 1)].reshape(32, 16, 128).astype(BF16)


def norm_kernel(product_ref, scaled_ref, grad_ref):
    count = product_ref.shape[0]

    def load(c):
        return product_ref[c].astype(F32)

    zeros = jnp.zeros(product_ref.shape[1:], F32)
    first = load(0)

    def sums(c, carry):
        off, scaled = load(c) - first, scaled_ref[c]
        return carry[0] + off, carry[1] + off * off, carry[2] + scaled, carry[3] + scaled * off

    total, square, scaled_total, cross = lax.fori_loop(0, count, sums, (zeros,) * 4, unroll=8)
    off_mean = total * (1.0 / count)
    mean = first + off_mean
    scaled_mean = scaled_total * (1.0 / count)
    square = jnp.maximum(square - off_mean * total, 0.0)
    cross = cross - off_mean * scaled_total
    inv_std = lax.rsqrt(square * (1.0 / count) + norm_eps)
    slope = inv_std * inv_std * cross * (1.0 / count)

    def write(c, carry):
        center = load(c) - mean
        grad_ref[c] = (inv_std * (scaled_ref[c] - scaled_mean - center * slope)).astype(BF16)
        return carry

    lax.fori_loop(0, count, write, 0, unroll=8)


def vmem():
    return pl.BlockSpec(memory_space=pltpu.VMEM)


def smem():
    return pl.BlockSpec(memory_space=pltpu.SMEM)


def shape(dims, dtype):
    return jax.ShapeDtypeStruct(dims, dtype)


def call(kernel, outs, operands, scratch=(), flops=0, scalars=1, aliases=None):
    moved = sum(o.size * o.dtype.itemsize for o in (*operands, *outs))
    return pl.pallas_call(
        kernel,
        out_shape=outs,
        in_specs=[smem()] * scalars + [vmem()] * (len(operands) - scalars),
        out_specs=[vmem()] * len(outs),
        scratch_shapes=scratch,
        input_output_aliases=aliases or {},
        compiler_params=pltpu.CompilerParams(vmem_limit_bytes=VMEM_LIMIT),
        cost_estimate=pl.CostEstimate(flops=flops, bytes_accessed=moved, transcendentals=0),
    )(*operands)


def swap(x, axis):
    return lax.ppermute(x, axis, [(0, 1), (1, 0)])


def swap_pair(x, core):
    at = [2 * bit + core for bit in range(2)]
    return lax.ppermute(x, (PAIR, "c"), [(at[0], at[1]), (at[1], at[0])])


def to_owners(x):
    return lax.all_to_all(x, OWNERS, split_axis=0, concat_axis=0, tiled=True)


def on_device(left, right, gate_out, out_grad, norm_gain, out_weight, token_mask):
    core = lax.axis_index("c")
    place = jnp.stack([lax.axis_index(PAIR), core]).astype(jnp.int32)
    pair = lax.axis_index(PAIR)
    both = to_owners(jnp.concatenate([left, right], axis=1))

    tokens = token_mask.astype(BF16)
    i_mask = lax.dynamic_index_in_dim(tokens.reshape(16, 2, 32), pair, 1, keepdims=False).reshape(512, 1)
    halves = tokens.reshape(4, 2, 128)
    mine_mask = lax.dynamic_index_in_dim(halves, core, 1, keepdims=False).reshape(512)
    other_mask = lax.dynamic_index_in_dim(halves, 1 - core, 1, keepdims=False).reshape(512)
    i_mask = jnp.broadcast_to(i_mask, (512, 128))
    j_mask = jnp.broadcast_to(mine_mask[:, None], (512, 128))
    k_mask = jnp.broadcast_to(jnp.concatenate([mine_mask, other_mask])[None], (16, 1024))
    row_mask = lax.dynamic_slice_in_dim(tokens, lax.axis_index(ROW) * 16, 16)
    col_mask = lax.dynamic_slice_in_dim(tokens, lax.axis_index(COL) * 128, 128)
    tile_mask = (row_mask[:, None] * col_mask[None, :])[None]
    gated_grad = (gate_out.astype(F32) * out_grad.astype(F32)).astype(BF16)
    linear = jnp.dot(
        out_weight, gated_grad.reshape(gated_grad.shape[0], -1), preferred_element_type=F32
    )
    scaled = norm_gain[:, None, None] * linear.reshape(left.shape)
    both, i_mask, j_mask, k_mask, tile_mask, scaled = lax.optimization_barrier(
        (both, i_mask, j_mask, k_mask, tile_mask, scaled)
    )

    half = (16, 4, 16, 128)
    rows = both.reshape(4, 2, 4, 4, 32, 128)[:, :, :, :, 16:, :]
    mine = lax.dynamic_index_in_dim(rows, core, 1, keepdims=False).reshape(half)
    other = swap(lax.dynamic_index_in_dim(rows, 1 - core, 1, keepdims=False).reshape(half), "c")
    near = jnp.stack([mine, other])
    far_1 = swap_pair(near, 1)
    both = both.reshape(32, 4, 32, 128)
    left_low, left_high, near = lax.optimization_barrier((both[:16, :, :16, :], both[16:, :, :16, :], near))
    left_low, left_high = swap(left_low, "c"), swap(left_high, "c")
    left_whole, right_near = call(
        near_kernel,
        [shape((512, 1024), BF16), shape((4, 2, 2, 2, 16, 1024), BF16)],
        [place, i_mask, j_mask, k_mask, both, left_low, left_high, near],
    )
    near_0, far_1, left_whole, right_near = lax.optimization_barrier((near, far_1, left_whole, right_near))
    far_0 = swap_pair(near_0, 0)

    flops = 2 * 512 * 512 * 1024
    blocks = (32, 4, 16, 128)
    product, right_whole = call(
        product_kernel,
        [shape(blocks, BF16), shape((4, 2, 2, 2, 16, 1024), BF16)],
        [place, j_mask, left_whole, far_0, far_1, right_near],
        aliases={5: 1},
        flops=flops,
    )
    product = to_owners(product.reshape(left.shape))
    (grad,) = call(
        norm_kernel,
        [shape(left.shape, BF16)],
        [product, scaled],
        flops=20 * product.size,
        scalars=0,
    )
    grad = to_owners(grad).reshape(blocks)

    half = (16, 4, 16, 128)
    right_send, right_keep = call(
        right_grad_kernel,
        [shape((2, *half), BF16), shape((2, *half), F32)],
        [place, left_whole, grad],
        flops=flops,
    )
    got_1 = swap_pair(right_send, 1)
    left_send, left_keep = call(
        left_grad_kernel, [shape(blocks, BF16), shape(blocks, F32)], [place, grad, right_whole], flops=flops
    )
    left_got = swap(left_send, "c")
    right_send, got_1 = lax.optimization_barrier((right_send, got_1))
    got_0 = swap_pair(right_send, 0)
    left_sum = (left_keep + left_got.astype(F32)).astype(BF16)
    left_sum, got_0 = lax.optimization_barrier((left_sum, got_0))
    left_home = to_owners(left_sum.reshape(left.shape))
    total = (right_keep + got_1.astype(F32) + got_0.astype(F32)).astype(BF16).reshape(2, 4, 4, 4, 16, 128)
    across = swap(total[1], "c")
    right_sum = jnp.where(
        core == 0, jnp.stack([total[0], across], axis=1), jnp.stack([across, total[0]], axis=1)
    )
    right_home = to_owners(right_sum.reshape(left.shape))
    return (left_home * tile_mask, right_home * tile_mask)


def solution(mesh):
    fine = Mesh(mesh.devices.reshape(SIZES), AXES)
    tile = P(None, ROW, COL)
    return jax.shard_map(
        on_device,
        mesh=fine,
        in_specs=(tile, tile, tile, tile, P(), P(), P()),
        out_specs=(tile, tile),
        check_vma=False,
    )
```

```python
import jax
import jax.numpy as jnp
from jax import lax
from jax.experimental import pallas as pl
from jax.experimental.pallas import tpu as pltpu
from jax.sharding import Mesh, PartitionSpec as P

norm_eps = 1e-05

AXES = ("zl", "y", "xh", "xl", "zh", "c")
SIZES = (4, 4, 2, 2, 4, 2)
ROW = ("zl", "y", "xh", "xl")
COL = ("zh", "c")
PAIR = "xh"
OWNERS = ("zl", "y", "xl", "zh")
BF16 = jnp.bfloat16
F32 = jnp.float32
VMEM_LIMIT = 32 * 1024 * 1024


def lanes(z, half=0):
    return slice(512 * half + 128 * z, 512 * half + 128 * (z + 1))


def place_rows(bit, halves, j_mask_ref, right_ref):
    j_masks = j_mask_ref[...].reshape(4, 2, 2, 2, 16, 128)
    mask = jnp.where(bit == 0, j_masks[:, :, 0], j_masks[:, :, 1])
    for z in range(4):
        for half in range(2):
            rows = halves[half, :, z, :, :].reshape(4, 2, 2, 16, 128)
            right_ref[:, :, bit, :, :, lanes(z, half)] = rows * mask


def near_kernel(
    place_ref, i_mask_ref, j_mask_ref, k_mask_ref, both_ref, left_low_ref, left_high_ref, near_ref, out_ref, right_ref
):
    parts = [both_ref[:, z, 0:16, :].reshape(512, 128) for z in range(4)]
    for z in range(4):
        ends = [ref[:, z, :, :].reshape(256, 128) for ref in (left_low_ref, left_high_ref)]
        parts.append(jnp.concatenate(ends, axis=0))
    i_mask = i_mask_ref[...].reshape(32, 16, 128)
    for n, part in enumerate(parts):
        cols = slice(128 * n, 128 * (n + 1))
        mask = (i_mask * k_mask_ref[:, cols][None]).reshape(512, 128)
        out_ref[:, cols] = part * mask
    place_rows(place_ref[0], near_ref, j_mask_ref, right_ref)


def whole_grad(grad_ref):
    return jnp.concatenate([grad_ref[:, z, :, :].reshape(512, 128) for z in range(4)], axis=1)


def product_kernel(place_ref, j_mask_ref, left_ref, far_0_ref, far_1_ref, right_in_ref, out_ref, right_ref):
    pair, core = place_ref[0], place_ref[1]
    del right_in_ref

    @pl.when(core == 0)
    def _():
        place_rows(1 - pair, far_0_ref, j_mask_ref, right_ref)

    @pl.when(core == 1)
    def _():
        place_rows(1 - pair, far_1_ref, j_mask_ref, right_ref)

    product = lax.dot_general(
        left_ref[...],
        right_ref[...].reshape(512, 1024),
        (((1,), (1,)), ((), ())),
        preferred_element_type=F32,
    )
    for z in range(4):
        out_ref[:, z, :, :] = product[:, lanes(z)].reshape(32, 16, 128).astype(BF16)


def right_grad_kernel(
    place_ref, left_ref, grad_ref, send_ref, keep_ref
):
    pair = place_ref[0]
    part = lax.dot_general(
        whole_grad(grad_ref),
        left_ref[...],
        (((0,), (0,)), ((), ())),
        preferred_element_type=F32,
    ).reshape(8, 2, 2, 16, 1024)
    send = jnp.where(pair == 0, part[:, 1], part[:, 0]).astype(BF16)
    keep = jnp.where(pair == 0, part[:, 0], part[:, 1])
    for z in range(4):
        for half in range(2):
            cols = lanes(z, half)
            send_ref[half, :, z, :, :] = send[..., cols].reshape(16, 16, 128)
            keep_ref[half, :, z, :, :] = keep[..., cols].reshape(16, 16, 128)


def left_grad_kernel(place_ref, grad_ref, right_ref, send_ref, keep_ref):
    part = jnp.dot(
        whole_grad(grad_ref), right_ref[...].reshape(512, 1024), preferred_element_type=F32
    )
    for z in range(4):
        keep_ref[:, z, :, :] = part[:, lanes(z)].reshape(32, 16, 128)
        send_ref[:, z, :, :] = part[:, lanes(z, 1)].reshape(32, 16, 128).astype(BF16)


def norm_kernel(product_ref, scaled_ref, grad_ref):
    count = product_ref.shape[0]

    def load(c):
        return product_ref[c].astype(F32)

    zeros = jnp.zeros(product_ref.shape[1:], F32)

    def sums(c, carry):
        return carry[0] + load(c), carry[1] + scaled_ref[c]

    total, scaled_total = lax.fori_loop(0, count, sums, (zeros, zeros), unroll=8)
    mean = total * (1.0 / count)
    scaled_mean = scaled_total * (1.0 / count)

    def squares(c, carry):
        center = load(c) - mean
        return carry[0] + center * center, carry[1] + scaled_ref[c] * center

    square, cross = lax.fori_loop(0, count, squares, (zeros, zeros), unroll=8)
    inv_std = lax.rsqrt(square * (1.0 / count) + norm_eps)
    slope = inv_std * inv_std * cross * (1.0 / count)

    def write(c, carry):
        center = load(c) - mean
        grad_ref[c] = (inv_std * (scaled_ref[c] - scaled_mean - center * slope)).astype(BF16)
        return carry

    lax.fori_loop(0, count, write, 0, unroll=8)


def vmem():
    return pl.BlockSpec(memory_space=pltpu.VMEM)


def smem():
    return pl.BlockSpec(memory_space=pltpu.SMEM)


def shape(dims, dtype):
    return jax.ShapeDtypeStruct(dims, dtype)


def call(kernel, outs, operands, scratch=(), flops=0, scalars=1, aliases=None):
    moved = sum(o.size * o.dtype.itemsize for o in (*operands, *outs))
    return pl.pallas_call(
        kernel,
        out_shape=outs,
        in_specs=[smem()] * scalars + [vmem()] * (len(operands) - scalars),
        out_specs=[vmem()] * len(outs),
        scratch_shapes=scratch,
        input_output_aliases=aliases or {},
        compiler_params=pltpu.CompilerParams(vmem_limit_bytes=VMEM_LIMIT),
        cost_estimate=pl.CostEstimate(flops=flops, bytes_accessed=moved, transcendentals=0),
    )(*operands)


def swap(x, axis):
    return lax.ppermute(x, axis, [(0, 1), (1, 0)])


def swap_pair(x, core):
    at = [2 * bit + core for bit in range(2)]
    return lax.ppermute(x, (PAIR, "c"), [(at[0], at[1]), (at[1], at[0])])


def to_owners(x):
    return lax.all_to_all(x, OWNERS, split_axis=0, concat_axis=0, tiled=True)


def on_device(left, right, gate_out, out_grad, norm_gain, out_weight, token_mask):
    core = lax.axis_index("c")
    place = jnp.stack([lax.axis_index(PAIR), core]).astype(jnp.int32)
    pair = lax.axis_index(PAIR)
    both = to_owners(jnp.concatenate([left, right], axis=1))

    tokens = token_mask.astype(BF16)
    i_mask = lax.dynamic_index_in_dim(tokens.reshape(16, 2, 32), pair, 1, keepdims=False).reshape(512, 1)
    halves = tokens.reshape(4, 2, 128)
    mine_mask = lax.dynamic_index_in_dim(halves, core, 1, keepdims=False).reshape(512)
    other_mask = lax.dynamic_index_in_dim(halves, 1 - core, 1, keepdims=False).reshape(512)
    i_mask = jnp.broadcast_to(i_mask, (512, 128))
    j_mask = jnp.broadcast_to(mine_mask[:, None], (512, 128))
    k_mask = jnp.broadcast_to(jnp.concatenate([mine_mask, other_mask])[None], (16, 1024))
    row_mask = lax.dynamic_slice_in_dim(tokens, lax.axis_index(ROW) * 16, 16)
    col_mask = lax.dynamic_slice_in_dim(tokens, lax.axis_index(COL) * 128, 128)
    tile_mask = (row_mask[:, None] * col_mask[None, :])[None]
    gated_grad = (gate_out.astype(F32) * out_grad.astype(F32)).astype(BF16)
    linear = jnp.dot(
        out_weight, gated_grad.reshape(gated_grad.shape[0], -1), preferred_element_type=F32
    )
    scaled = norm_gain[:, None, None] * linear.reshape(left.shape)
    both, i_mask, j_mask, k_mask, tile_mask, scaled = lax.optimization_barrier(
        (both, i_mask, j_mask, k_mask, tile_mask, scaled)
    )

    half = (16, 4, 16, 128)
    rows = both.reshape(4, 2, 4, 4, 32, 128)[:, :, :, :, 16:, :]
    mine = lax.dynamic_index_in_dim(rows, core, 1, keepdims=False).reshape(half)
    other = swap(lax.dynamic_index_in_dim(rows, 1 - core, 1, keepdims=False).reshape(half), "c")
    near = jnp.stack([mine, other])
    far_1 = swap_pair(near, 1)
    both = both.reshape(32, 4, 32, 128)
    left_low, left_high, near = lax.optimization_barrier((both[:16, :, :16, :], both[16:, :, :16, :], near))
    left_low, left_high = swap(left_low, "c"), swap(left_high, "c")
    left_whole, right_near = call(
        near_kernel,
        [shape((512, 1024), BF16), shape((4, 2, 2, 2, 16, 1024), BF16)],
        [place, i_mask, j_mask, k_mask, both, left_low, left_high, near],
    )
    near_0, far_1, left_whole, right_near = lax.optimization_barrier((near, far_1, left_whole, right_near))
    far_0 = swap_pair(near_0, 0)

    flops = 2 * 512 * 512 * 1024
    blocks = (32, 4, 16, 128)
    product, right_whole = call(
        product_kernel,
        [shape(blocks, BF16), shape((4, 2, 2, 2, 16, 1024), BF16)],
        [place, j_mask, left_whole, far_0, far_1, right_near],
        aliases={5: 1},
        flops=flops,
    )
    product = to_owners(product.reshape(left.shape))
    (grad,) = call(
        norm_kernel,
        [shape(left.shape, BF16)],
        [product, scaled],
        flops=20 * product.size,
        scalars=0,
    )
    grad = to_owners(grad).reshape(blocks)

    half = (16, 4, 16, 128)
    right_send, right_keep = call(
        right_grad_kernel,
        [shape((2, *half), BF16), shape((2, *half), F32)],
        [place, left_whole, grad],
        flops=flops,
    )
    got_1 = swap_pair(right_send, 1)
    left_send, left_keep = call(
        left_grad_kernel, [shape(blocks, BF16), shape(blocks, F32)], [place, grad, right_whole], flops=flops
    )
    left_got = swap(left_send, "c")
    right_send, got_1 = lax.optimization_barrier((right_send, got_1))
    got_0 = swap_pair(right_send, 0)
    left_sum = (left_keep + left_got.astype(F32)).astype(BF16)
    left_sum, got_0 = lax.optimization_barrier((left_sum, got_0))
    left_home = to_owners(left_sum.reshape(left.shape))
    total = (right_keep + got_1.astype(F32) + got_0.astype(F32)).astype(BF16).reshape(2, 4, 4, 4, 16, 128)
    across = swap(total[1], "c")
    right_sum = jnp.where(
        core == 0, jnp.stack([total[0], across], axis=1), jnp.stack([across, total[0]], axis=1)
    )
    right_home = to_owners(right_sum.reshape(left.shape))
    return (left_home * tile_mask, right_home * tile_mask)


def solution(mesh):
    fine = Mesh(mesh.devices.reshape(SIZES), AXES)
    tile = P(None, ROW, COL)
    return jax.shard_map(
        on_device,
        mesh=fine,
        in_specs=(tile, tile, tile, tile, P(), P(), P()),
        out_specs=(tile, tile),
        check_vma=False,
    )
```
